256 devices in a mesh: gx: 8 (over y, core), gy: 8 (over x, z_hi), gz: 4 (over z_lo).
Axes of the slice: x: 4, y: 4, z: 8 (z_hi: 2, z_lo: 4; z = z_hi * 4 + z_lo), core: 2. Of those that a mesh axis runs over, the one named last changes fastest.
Arguments:
- pressure: float32 [256, 256, 512], P('gx', 'gy', 'gz'), may hold values from -6 to 6
- pressure_prev: float32 [256, 256, 512], P('gx', 'gy', 'gz'), may hold values from -6 to 6
- horiz_coef: float32 [256, 256, 512], P('gx', 'gy', 'gz'), may hold values from 0.04 to 0.19
- vert_coef: float32 [256, 256, 512], P('gx', 'gy', 'gz'), may hold values from 0.04 to 0.19
- traces: bfloat16 [256, 64, 2, 128], P(('gx', 'gy', 'gz')), may hold values from -6 to 6
- recv_cell: int32 [256, 64, 2], P(('gx', 'gy', 'gz')), may hold values from 0 to 131071, as said below
- recv_owner: int32 [256, 64, 2], P(('gx', 'gy', 'gz')), may hold values from 0 to 3, as said below
- trace_counts: int32 [256, 64], P(('gx', 'gy', 'gz')), may hold values from 0 to 2, as said below
Outputs:
- final_pressure: float32 [256, 256, 512], P('gx', 'gy', 'gz')
- final_prev: float32 [256, 256, 512], P('gx', 'gy', 'gz')
The draws below stay inside these ranges and needn't reach their ends.
Inputs may be any that keep to these rules, and one draw needn't show every extreme that they name: `recv_cell`: flat index of a cell inside the 32 x 32 x 128 block of the owning subdomain, inline slowest. `recv_owner`: depth index of the owning subdomain within the destination column. `trace_counts`: slots at and past the count are unused; some column receives 2 slots from every holder in every draw.
All inputs are finite; a program needn't handle non-finite values.
Results may differ from the reference program's by a relative error of at most 0.00044.
Values may be sent and summed in bfloat16 or wider, within the bound.
A program may use at most 128 MiB of HBM per device.

```python
import math
import jax
import jax.numpy as jnp
from jax import lax

CX = 32
CY = 32
CZ = 128
STEPS = 32
TSAMP = 128
SUB = 4
CAP = 2
COLS = 64
SOURCES = 256
NX = 256
NY = 256
NZ = 512
N_GY = 8
N_GZ = 4


def draw_recv_cell(key, part):
    return jax.random.randint(jax.random.fold_in(key, 11), (SOURCES, COLS, CAP), 0, CX * CY * CZ, dtype=jnp.int32)


def draw_recv_owner(key, part):
    return jax.random.randint(jax.random.fold_in(key, 12), (SOURCES, COLS, CAP), 0, N_GZ, dtype=jnp.int32)


def draw_trace_counts(key, part):
    base = jax.random.randint(jax.random.fold_in(key, 13), (SOURCES, COLS), 0, CAP + 1, dtype=jnp.int32)
    full_col = jax.random.randint(jax.random.fold_in(key, 14), (), 0, COLS, dtype=jnp.int32)
    columns = jnp.arange(COLS, dtype=jnp.int32)[None, :]
    return jnp.where(columns == full_col, CAP, base).astype(jnp.int32)


def steps_of(own_key, shape, pieces, least, high):
    gain = 1.0
    for dim, shards_of in pieces:
        heights = jax.random.uniform(jax.random.fold_in(jax.random.fold_in(own_key, 6), dim), (shards_of,), jnp.float32, least / len(pieces), high / len(pieces))
        gain = gain * jnp.repeat(jnp.exp(heights), shape[dim] // shards_of).reshape((-1,) + (1,) * (len(shape) - 1 - dim))
    return gain


def centred(own_key, extent, scale, bound, cuts=(), held_as=jnp.bfloat16):
    drawn = scale * jax.random.normal(own_key, extent, jnp.float32)
    if cuts:
        drawn = drawn * steps_of(own_key, extent, cuts, -0.22, 0.18)
    return jnp.clip(drawn, -bound, bound).astype(held_as)


def setup_inputs(seed: int = 0) -> dict:
    keys = jax.random.split(jax.random.key(seed), 9)
    return {
        "pressure": centred(keys[0], (NX, NY, NZ), 1.0, 6.0, ((0, 8), (1, 8), (2, 4)), jnp.float32),
        "pressure_prev": centred(keys[1], (NX, NY, NZ), 1.0, 6.0, ((0, 8), (1, 8), (2, 4)), jnp.float32),
        "horiz_coef": jnp.clip(jnp.exp(math.log(0.19) - 1.5581446 * jax.random.uniform(keys[2], (NX, NY, NZ), jnp.float32) ** steps_of(keys[2], (NX, NY, NZ), ((0, 8), (1, 8), (2, 4)), -0.2, 0.2)), 0.04, 0.19),
        "vert_coef": jnp.clip(jnp.exp(math.log(0.19) - 1.5581446 * jax.random.uniform(keys[3], (NX, NY, NZ), jnp.float32) ** steps_of(keys[3], (NX, NY, NZ), ((0, 8), (1, 8), (2, 4)), -0.2, 0.2)), 0.04, 0.19),
        "traces": centred(keys[4], (SOURCES, COLS, CAP, TSAMP), 1.0, 6.0, ((0, 256),)),
        "recv_cell": draw_recv_cell(jax.random.fold_in(keys[8], 71), 0),
        "recv_owner": draw_recv_owner(jax.random.fold_in(keys[8], 71), 0),
        "trace_counts": draw_trace_counts(jax.random.fold_in(keys[8], 71), 0),
    }


COEF = (-205.0 / 72.0, 8.0 / 5.0, -1.0 / 5.0, 8.0 / 315.0, -1.0 / 560.0)


def laplace_terms(padded):
    sa, sb, sc = padded.shape
    na, nb, nc = sa - 8, sb - 8, sc - 8
    center = padded[4:4 + na, 4:4 + nb, 4:4 + nc]
    lxx = COEF[0] * center
    lyy = COEF[0] * center
    lzz = COEF[0] * center
    for k in range(1, 5):
        lxx = lxx + COEF[k] * (padded[4 + k:4 + k + na, 4:4 + nb, 4:4 + nc] + padded[4 - k:4 - k + na, 4:4 + nb, 4:4 + nc])
        lyy = lyy + COEF[k] * (padded[4:4 + na, 4 + k:4 + k + nb, 4:4 + nc] + padded[4:4 + na, 4 - k:4 - k + nb, 4:4 + nc])
        lzz = lzz + COEF[k] * (padded[4:4 + na, 4:4 + nb, 4 + k:4 + k + nc] + padded[4:4 + na, 4:4 + nb, 4 - k:4 - k + nc])
    return center, lxx + lyy, lzz


def reference(pressure, pressure_prev, horiz_coef, vert_coef, traces, recv_cell, recv_owner, trace_counts):
    box_table = (jnp.arange(TSAMP, dtype=jnp.int32)[:, None] // SUB == STEPS - 1 - jnp.arange(STEPS, dtype=jnp.int32)[None, :]).astype(jnp.bfloat16)
    amps = jnp.dot(traces.reshape(-1, TSAMP), box_table, preferred_element_type=jnp.float32).astype(jnp.bfloat16)
    column = jnp.broadcast_to(jnp.arange(COLS, dtype=jnp.int32)[None, :, None], recv_cell.shape).reshape(-1)
    slots = jnp.broadcast_to(jnp.arange(CAP, dtype=jnp.int32)[None, None, :], recv_cell.shape)
    live = (slots < trace_counts[:, :, None]).reshape(-1)
    cells = recv_cell.reshape(-1)
    xs = (column // N_GY) * CX + cells // (CY * CZ)
    ys = (column % N_GY) * CY + (cells // CZ) % CY
    zs = recv_owner.reshape(-1) * CZ + cells % CZ
    weight = jnp.where(live, 1.0, 0.0).astype(jnp.float32)

    def advance(step, carry):
        field, older = carry
        amp_now = lax.dynamic_index_in_dim(amps, step, 1, keepdims=False).astype(jnp.float32) * weight
        source = jnp.zeros((NX, NY, NZ), jnp.float32).at[xs, ys, zs].add(amp_now)
        center, lhor, lver = laplace_terms(jnp.pad(field, 4))
        fresh = 2.0 * center - older + horiz_coef * lhor + vert_coef * lver + source
        return (fresh, field)

    final_pressure, final_prev = lax.fori_loop(0, STEPS, advance, (pressure, pressure_prev))
    return final_pressure, final_prev
```

```python
import functools

import jax
import jax.numpy as jnp
from jax import lax
from jax.experimental import pallas as pl
from jax.experimental.pallas import tpu as pltpu
from jax.sharding import PartitionSpec as P

STEPS = 32
MESH = pl.DeviceIdType.MESH
COEF = (-205.0 / 72.0, 8.0 / 5.0, -1.0 / 5.0, 8.0 / 315.0, -1.0 / 560.0)
SCALE = 5040.0
TAPS = (8064.0, -1008.0, 128.0, -9.0)

NY = 64
CHUNK = 16
NCH = NY // CHUNK
ROWS = CHUNK * 32
SLAB = 32
FIELD = (NY + 8) * SLAB
F32, BF16 = jnp.float32, jnp.bfloat16


def taps(distance):
    value = jnp.zeros(distance.shape, F32)
    for k in range(1, 5):
        value = jnp.where(distance == k, TAPS[k - 1], value)
    return value


def iota(shape, dim):
    return lax.broadcasted_iota(jnp.int32, shape, dim)


def kernel(
    p_ref, q_ref, h_ref, v_ref, f_ref, outp_ref, outq_ref,
    fld, hc, vc, kc, hl, hot, zhot, wgt, xs, xh, hb, zs, zh, place, raw, band, zout, zin,
    ysend, yrecv, xsend, xrecv, zsend, zrecv, psend, precv,
):
    gx, gy, gz = lax.axis_index("gx"), lax.axis_index("gy"), lax.axis_index("gz")
    nx, ny, nz = lax.axis_size("gx"), lax.axis_size("gy"), lax.axis_size("gz")
    half = lax.rem(gy, 2)
    partner = gy + 1 - 2 * half
    has = {
        ("x", 0): gx > 0, ("x", 1): gx < nx - 1,
        ("y", 0): gy > 1, ("y", 1): gy < ny - 2,
        ("z", 0): gz > 0, ("z", 1): gz < nz - 1,
    }
    peer = {
        ("x", 0): {"gx": gx - 1}, ("x", 1): {"gx": gx + 1},
        ("y", 0): {"gy": gy - 2}, ("y", 1): {"gy": gy + 2},
        ("z", 0): {"gz": gz - 1}, ("z", 1): {"gz": gz + 1},
    }

    def clear(ref, start, count):
        ref[pl.ds(start, count), :] = jnp.zeros((count, 128), F32)

    for par in range(2):
        clear(fld, par * FIELD, 4 * SLAB)
        clear(fld, par * FIELD + (NY + 4) * SLAB, 4 * SLAB)
    zh[...] = jnp.zeros_like(zh)

    barrier = pltpu.get_barrier_semaphore()
    pl.semaphore_signal(barrier, inc=1, device_id={"gy": partner}, device_id_type=MESH)
    greet = jnp.int32(1)
    for key, ok in has.items():

        @pl.when(ok)
        def _(key=key):
            pl.semaphore_signal(barrier, inc=1, device_id=peer[key], device_id_type=MESH)

        greet = greet + ok.astype(jnp.int32)
    pl.semaphore_wait(barrier, greet)

    def pair(n):
        return pltpu.make_async_remote_copy(
            src_ref=(p_ref, q_ref, h_ref, v_ref)[n],
            dst_ref=raw.at[n],
            send_sem=psend.at[n],
            recv_sem=precv.at[n],
            device_id={"gy": partner},
            device_id_type=MESH,
        )

    for n in range(4):
        pair(n).start()

    @pl.loop(0, NCH)
    def _(c):
        clear(hb, pl.multiple_of(c * ROWS, ROWS), ROWS)

    band[...] = taps(jnp.abs(lax.rem(iota((256, 128), 0), 128) - iota((256, 128), 1))).astype(BF16)
    row, depth = iota((16, 256), 0), lax.rem(iota((16, 256), 1), 128)
    m = lax.rem(row, 4)
    away = jnp.where(row < 8, 128 + m - depth, depth + 4 - m)
    upper = lax.rem(row, 8) >= 4
    value = taps(away)
    zout[0] = jnp.where(upper, 0.0, value).astype(BF16)
    zout[1] = jnp.where(upper, value, 0.0).astype(BF16)
    row, lane = lax.rem(iota((32, 128), 0), 16), iota((32, 128), 1)
    target = lax.rem(row, 4) + jnp.where(row >= 8, 124, 0)
    upper = lax.rem(row, 8) >= 4
    hit = lane == target
    zin[0] = jnp.where(hit & jnp.logical_not(upper), 1.0, 0.0).astype(BF16)
    zin[1] = jnp.where(hit & upper, 1.0, 0.0).astype(BF16)

    for col in range(2):
        packed = f_ref[col]
        for k in range(2):
            pick = iota((8, 128), 1) == 64 * k + 32 + iota((8, 128), 0)
            by_lane = lax.dot_general(
                jnp.where(pick, 1.0, 0.0).astype(BF16), packed,
                (((1,), (1,)), ((), ())), preferred_element_type=F32,
            )
            where = (by_lane[0:1] * 32.0 + by_lane[1:2]).astype(jnp.int32)
            mine = by_lane[3:4].astype(jnp.int32) == gz
            where = jnp.where(mine, where, -1)
            for block in range(4):
                at = iota((256, 256), 0) + block * 256
                hot[pl.ds(col * 1024 + block * 256, 256), pl.ds(k * 256, 256)] = jnp.where(
                    at == where, 1.0, 0.0
                ).astype(BF16)
            spread = jnp.where(iota((128, 128), 0) == 64 * k + 34, 1.0, 0.0).astype(BF16)
            z = jnp.dot(packed, spread, preferred_element_type=F32).astype(jnp.int32)
            zhot[pl.ds(col * 512 + k * 256, 256), :] = jnp.where(
                z == iota((256, 128), 1), 1.0, 0.0
            )

    def arrange(refs, first):
        @pl.loop(0, 32)
        def _(y):
            for j in range(4):
                take = pl.ds(j * 32 + y, 8, stride=128)
                put = pl.multiple_of((first + y) * SLAB + j * 8, 8)
                fld[pl.ds(put + 4 * SLAB, 8), :] = refs[0][take, :]
                fld[pl.ds(put + 4 * SLAB + FIELD, 8), :] = refs[1][take, :]
                h, v = refs[2][take, :], refs[3][take, :]
                hc[pl.ds(put, 8), :] = h
                vc[pl.ds(put, 8), :] = v * (1.0 / SCALE)
                kc[pl.ds(put, 8), :] = 2.0 + COEF[0] * (2.0 * h + v)

    arrange((p_ref, q_ref, h_ref, v_ref), 32 * half)
    for n in range(4):
        pair(n).wait_recv()
    arrange([raw.at[n] for n in range(4)], 32 - 32 * half)

    def y_copy(side, par):
        src = par * FIELD + (4 if side == 0 else NY) * SLAB
        dst = par * FIELD + (NY + 4 if side == 0 else 0) * SLAB
        return pltpu.make_async_remote_copy(
            src_ref=fld.at[pl.ds(pl.multiple_of(src, 128), 128)],
            dst_ref=fld.at[pl.ds(pl.multiple_of(dst, 128), 128)],
            send_sem=ysend.at[side],
            recv_sem=yrecv.at[1 - side, par],
            device_id=peer["y", side],
            device_id_type=MESH,
        )

    def y_wait(side, par):
        here = pl.ds(pl.multiple_of(par * FIELD + (0 if side == 0 else NY + 4) * SLAB, 128), 128)
        pltpu.make_async_remote_copy(
            src_ref=fld.at[here], dst_ref=fld.at[here], send_sem=ysend.at[side],
            recv_sem=yrecv.at[side, par], device_id=peer["y", side], device_id_type=MESH,
        ).wait_recv()

    def x_copy(side, c, par, there):
        rows = pl.ds(pl.multiple_of(c * CHUNK * 4, 64), CHUNK * 4)
        return pltpu.make_async_remote_copy(
            src_ref=xs.at[side, rows],
            dst_ref=xh.at[par, there, rows],
            send_sem=xsend.at[side, c],
            recv_sem=xrecv.at[there, par, c],
            device_id=peer["x", side],
            device_id_type=MESH,
        )

    def z_copy(side, c, par, there):
        return pltpu.make_async_remote_copy(
            src_ref=zs.at[c, pl.ds(8 - 8 * side, 8)],
            dst_ref=zh.at[par, c, pl.ds(8 * there, 8)],
            send_sem=zsend.at[side, c],
            recv_sem=zrecv.at[there, par, c],
            device_id=peer["z", side],
            device_id_type=MESH,
        )

    def settle(c):
        for side in range(2):

            @pl.when(has["x", side])
            def _():
                x_copy(side, c, 0, 1 - side).wait_send()

            @pl.when(has["z", side])
            def _():
                z_copy(side, c, 0, 1 - side).wait_send()

            @pl.when(has["y", side] & (c == (0 if side == 0 else NCH - 1)))
            def _():
                y_copy(side, 0).wait_send()

    def send(c, par):
        for side in range(2):

            @pl.when(has["y", side] & (c == (0 if side == 0 else NCH - 1)))
            def _():
                y_copy(side, par).start()

        first = par * FIELD + (4 + c * CHUNK) * SLAB
        rows = pl.ds(pl.multiple_of(c * CHUNK * 4, 64), CHUNK * 4)
        for side in range(2):
            xs[side, rows, :] = fld[pl.ds(first + 7 * side, CHUNK * 4, stride=8), :]

            @pl.when(has["x", side])
            def _():
                x_copy(side, c, par, 1 - side).start()

        start = pl.multiple_of(c * ROWS, ROWS)
        dims = (((1,), (1,)), ((), ()))
        zs[c] = lax.dot_general(
            zout[0], hl[pl.ds(start, 256), :], dims, preferred_element_type=F32
        ) + lax.dot_general(
            zout[1], hl[pl.ds(start + 256, 256), :], dims, preferred_element_type=F32
        )
        for side in range(2):

            @pl.when(has["z", side])
            def _():
                z_copy(side, c, par, 1 - side).start()

    def split(start, new):
        high = new.astype(BF16)
        hl[pl.ds(start, SLAB), 0:128] = high
        hl[pl.ds(start, SLAB), 128:256] = (new - high.astype(F32)).astype(BF16)

    @pl.loop(0, NCH)
    def _(i):
        c = jnp.where(i == 0, 0, jnp.where(i == 1, NCH - 1, i - 1))

        @pl.loop(0, CHUNK)
        def _(y):
            start = pl.multiple_of(c * ROWS + y * SLAB, SLAB)
            split(start, fld[pl.ds(start + 4 * SLAB, SLAB), :])

        send(c, 0)

    sub = iota((8, 128), 0)

    def step(t, carry):
        par = lax.rem(t, 2)
        old, now = (1 - par) * FIELD + 4 * SLAB, par * FIELD + 4 * SLAB

        for col in range(2):
            for k in range(2):
                spread = jnp.where(iota((128, 128), 0) == 64 * k + t, 1.0, 0.0).astype(BF16)
                amp = jnp.dot(f_ref[col], spread, preferred_element_type=F32)
                at = pl.ds(col * 512 + k * 256, 256)
                wgt[at, :] = (zhot[at, :] * amp).astype(BF16)

        @pl.loop(0, 2 * NCH)
        def _(b):
            r = pl.multiple_of(b * 256, 256)
            col = pl.multiple_of((b // NCH) * 512, 512)
            rows = pl.ds(r, 256)
            inner = jnp.dot(hl[rows, :], band[...], preferred_element_type=F32)
            source = jnp.dot(hot[rows, :], wgt[pl.ds(col, 512), :], preferred_element_type=F32)
            was = pl.ds(pl.multiple_of(old + r, 128), 256)
            fld[was, :] = (
                source
                - fld[was, :]
                + kc[rows, :] * fld[pl.ds(pl.multiple_of(now + r, 128), 256), :]
                + vc[rows, :] * inner
            )

        @pl.loop(0, NCH)
        def _(i):
            c = jnp.where(i == 0, 0, jnp.where(i == 1, NCH - 1, i - 1))
            first = pl.multiple_of(c * ROWS, ROWS)
            for side in range(2):

                @pl.when(has["y", side] & (c == (0 if side == 0 else NCH - 1)))
                def _():
                    y_wait(side, par)

                @pl.when(has["x", side])
                def _():
                    x_copy(side, c, par, side).wait_recv()
                    rows = pl.ds(pl.multiple_of(c * CHUNK * 4, 64), CHUNK * 4)
                    hb[pl.ds(first + 7 * side, CHUNK * 4, stride=8), :] = xh[par, side, rows, :]

                @pl.when(has["z", side])
                def _():
                    z_copy(side, c, par, side).wait_recv()

            got = zh[par, c]
            high = got.astype(BF16)
            both = jnp.concatenate([high, (got - high.astype(F32)).astype(BF16)], axis=0)
            for n in range(2):
                place[pl.ds(256 * n, 256), :] = lax.dot_general(
                    both, zin[n], (((0,), (0,)), ((), ())), preferred_element_type=F32
                )
            settle(c)

            @pl.loop(0, CHUNK)
            def _(y):
                at = pl.multiple_of(y * SLAB, SLAB)
                r = pl.multiple_of(first + y * SLAB, SLAB)
                base = pl.multiple_of(now + r, SLAB)
                mid = [fld[pl.ds(base + 8 * j, 8), :] for j in range(4)]
                edge = [hb[pl.ds(r + 8 * j, 8), :] for j in range(4)]
                below = [jnp.where(sub == 0, e, pltpu.roll(v, 1, 0)) for e, v in zip(edge, mid)]
                above = [jnp.where(sub == 7, e, pltpu.roll(v, 7, 0)) for e, v in zip(edge, mid)]
                line = below + mid + above
                tiles = []
                for j in range(4):
                    total = None
                    for k in range(1, 5):
                        near = (line[4 + j + k] + line[4 + j - k]) + (
                            fld[pl.ds(base + 8 * j + k * SLAB, 8), :]
                            + fld[pl.ds(base + 8 * j - k * SLAB, 8), :]
                        )
                        near = COEF[k] * near
                        total = near if total is None else total + near
                    here = pl.ds(r + 8 * j, 8)
                    was = pl.ds(pl.multiple_of(old + r, SLAB) + 8 * j, 8)
                    new = (
                        fld[was, :]
                        + hc[here, :] * total
                        + vc[here, :] * place[pl.ds(at + 8 * j, 8), :]
                    )
                    fld[was, :] = new
                    tiles.append(new)
                split(r, jnp.concatenate(tiles, axis=0))

            @pl.when(t < STEPS - 1)
            def _():
                send(c, 1 - par)

        return carry

    lax.fori_loop(0, STEPS, step, 0)
    for n in range(4):
        pair(n).wait_send()

    @pl.loop(0, 32)
    def _(y):
        for j in range(4):
            put = pl.ds(j * 32 + y, 8, stride=128)
            take = pl.multiple_of((4 + 32 * half + y) * SLAB + j * 8, 8)
            outp_ref[put, :] = fld[pl.ds(take, 8), :]
            outq_ref[put, :] = fld[pl.ds(take + FIELD, 8), :]


def body(
    pressure, pressure_prev, horiz_coef, vert_coef, traces, recv_cell, recv_owner, trace_counts
):
    samples = traces.shape[-1]
    columns, slots = recv_cell.shape[1:]
    per_step = samples // STEPS
    box_table = (
        jnp.arange(samples, dtype=jnp.int32)[:, None] // per_step
        == STEPS - 1 - jnp.arange(STEPS, dtype=jnp.int32)[None, :]
    ).astype(BF16)
    amps = jnp.dot(
        traces.reshape(-1, samples), box_table, preferred_element_type=F32
    ).astype(BF16).reshape(columns, slots, STEPS)
    cell = recv_cell[0]
    x, y, z = cell // 4096, (cell // 128) % 32, cell % 128
    live = jnp.arange(slots, dtype=jnp.int32)[None, :] < trace_counts[0][:, None]
    owner = jnp.where(live, recv_owner[0], -1)
    code = jnp.stack([y, (x % 4) * 8 + x // 4, z, owner], axis=-1).astype(BF16)
    packed = jnp.concatenate(
        [amps, code, jnp.zeros((columns, slots, 28), BF16)], axis=-1
    ).reshape(columns, 128)
    routed = lax.all_to_all(packed, ("gx", "gy"), split_axis=0, concat_axis=0, tiled=True)
    own = lax.all_gather(routed, "gz", axis=0, tiled=True)
    pairs = [(i, i ^ 1) for i in range(lax.axis_size("gy"))]
    other = lax.ppermute(own, "gy", pairs)
    low = lax.rem(lax.axis_index("gy"), 2) == 0
    table = jnp.stack([jnp.where(low, own, other), jnp.where(low, other, own)])

    flat = [a.reshape(1024, 128) for a in (pressure, pressure_prev, horiz_coef, vert_coef)]
    vmem = pl.BlockSpec(memory_space=pltpu.VMEM)
    dma = pltpu.SemaphoreType.DMA
    outs = pl.pallas_call(
        kernel,
        out_shape=[jax.ShapeDtypeStruct((1024, 128), F32)] * 2,
        in_specs=[vmem] * 5,
        out_specs=[vmem] * 2,
        scratch_shapes=[
            pltpu.VMEM((2 * FIELD, 128), F32),
            pltpu.VMEM((NY * SLAB, 128), F32),
            pltpu.VMEM((NY * SLAB, 128), F32),
            pltpu.VMEM((NY * SLAB, 128), F32),
            pltpu.VMEM((NY * SLAB, 256), BF16),
            pltpu.VMEM((NY * SLAB, 512), BF16),
            pltpu.VMEM((1024, 128), F32),
            pltpu.VMEM((1024, 128), BF16),
            pltpu.VMEM((2, NY * 4, 128), F32),
            pltpu.VMEM((2, 2, NY * 4, 128), F32),
            pltpu.VMEM((NY * SLAB, 128), F32),
            pltpu.VMEM((NCH, 16, 256), F32),
            pltpu.VMEM((2, NCH, 16, 256), F32),
            pltpu.VMEM((ROWS, 128), F32),
            pltpu.VMEM((4, 1024, 128), F32),
            pltpu.VMEM((256, 128), BF16),
            pltpu.VMEM((2, 16, 256), BF16),
            pltpu.VMEM((2, 32, 128), BF16),
            dma((2,)), dma((2, 2)),
            dma((2, NCH)), dma((2, 2, NCH)),
            dma((2, NCH)), dma((2, 2, NCH)),
            dma((4,)), dma((4,)),
        ],
        compiler_params=pltpu.CompilerParams(
            collective_id=0, has_side_effects=True, vmem_limit_bytes=40 * 1024 * 1024
        ),
    )(*flat, table)
    return tuple(o.reshape(32, 32, 128) for o in outs)


def solution(mesh):
    block = P("gx", "gy", "gz")
    placed = (
        block,
        block,
        block,
        block,
        P(("gx", "gy", "gz"), None, None, None),
        P(("gx", "gy", "gz"), None, None),
        P(("gx", "gy", "gz"), None, None),
        P(("gx", "gy", "gz"), None),
    )
    return jax.shard_map(
        body, mesh=mesh, in_specs=placed, out_specs=(block, block), check_vma=False
    )
```

```python
import functools

import jax
import jax.numpy as jnp
from jax import lax
from jax.experimental import pallas as pl
from jax.experimental.pallas import tpu as pltpu
from jax.sharding import PartitionSpec as P

STEPS = 32
MESH = pl.DeviceIdType.MESH
COEF = (-205.0 / 72.0, 8.0 / 5.0, -1.0 / 5.0, 8.0 / 315.0, -1.0 / 560.0)
SCALE = 5040.0
TAPS = (8064.0, -1008.0, 128.0, -9.0)

NY = 64
CHUNK = 16
NCH = NY // CHUNK
ROWS = CHUNK * 32
GROUP = 4
SLAB = 32
FIELD = (NY + 8) * SLAB
F32, BF16 = jnp.float32, jnp.bfloat16


def taps(distance):
    value = jnp.zeros(distance.shape, F32)
    for k in range(1, 5):
        value = jnp.where(distance == k, TAPS[k - 1], value)
    return value


def code(value):
    return jnp.round((value - 0.115) * (32767.0 / 0.075)).astype(jnp.int16)


def decode(value):
    return value.astype(jnp.int32).astype(F32) * (0.075 / 32767.0) + 0.115


def iota(shape, dim):
    return lax.broadcasted_iota(jnp.int32, shape, dim)


def kernel(
    p_ref, q_ref, h_ref, v_ref, op_ref, oq_ref, oh_ref, ov_ref, f_ref, outp_ref, outq_ref,
    fld, hc, vc, kc, hl, hot, zhot, wgt, xs, xh, hb, zs, zh, raw, band, lap, src,
    ysend, yrecv, xsend, xrecv, zsend, zrecv,
):
    gx, gy, gz = lax.axis_index("gx"), lax.axis_index("gy"), lax.axis_index("gz")
    nx, ny, nz = lax.axis_size("gx"), lax.axis_size("gy"), lax.axis_size("gz")
    half = lax.rem(gy, 2)
    has = {
        ("x", 0): gx > 0, ("x", 1): gx < nx - 1,
        ("y", 0): gy > 1, ("y", 1): gy < ny - 2,
        ("z", 0): gz > 0, ("z", 1): gz < nz - 1,
    }
    peer = {
        ("x", 0): {"gx": gx - 1}, ("x", 1): {"gx": gx + 1},
        ("y", 0): {"gy": gy - 2}, ("y", 1): {"gy": gy + 2},
        ("z", 0): {"gz": gz - 1}, ("z", 1): {"gz": gz + 1},
    }

    def clear(ref, start, count):
        ref[pl.ds(start, count), :] = jnp.zeros((count, 128), F32)

    for par in range(2):
        clear(fld, par * FIELD, 4 * SLAB)
        clear(fld, par * FIELD + (NY + 4) * SLAB, 4 * SLAB)
    zh[...] = jnp.zeros_like(zh)

    barrier = pltpu.get_barrier_semaphore()
    greet = jnp.int32(0)
    for key, ok in has.items():

        @pl.when(ok)
        def _(key=key):
            pl.semaphore_signal(barrier, inc=1, device_id=peer[key], device_id_type=MESH)

        greet = greet + ok.astype(jnp.int32)
    pl.semaphore_wait(barrier, greet)

    @pl.loop(0, NCH)
    def _(c):
        clear(hb, pl.multiple_of(c * ROWS, ROWS), ROWS)

    depth = lax.rem(iota((256, 128), 0), 128)
    band[:, 0:128] = taps(jnp.abs(depth - iota((256, 128), 1))).astype(BF16)
    m = lax.rem(iota((256, 128), 1), 8)
    band[:, 128:256] = taps(jnp.where(m < 4, 128 + m - depth, depth + 8 - m)).astype(BF16)

    for col in range(2):
        packed = f_ref[col]
        for k in range(2):
            pick = iota((8, 128), 1) == 64 * k + 32 + iota((8, 128), 0)
            by_lane = lax.dot_general(
                jnp.where(pick, 1.0, 0.0).astype(BF16), packed,
                (((1,), (1,)), ((), ())), preferred_element_type=F32,
            )
            where = (by_lane[0:1] * 32.0 + by_lane[1:2]).astype(jnp.int32)
            mine = by_lane[3:4].astype(jnp.int32) == gz
            where = jnp.where(mine, where, -1)
            for block in range(4):
                at = iota((256, 256), 0) + block * 256
                hot[pl.ds(col * 1024 + block * 256, 256), pl.ds(k * 256, 256)] = jnp.where(
                    at == where, 1.0, 0.0
                ).astype(BF16)
            spread = jnp.where(iota((128, 128), 0) == 64 * k + 34, 1.0, 0.0).astype(BF16)
            z = jnp.dot(packed, spread, preferred_element_type=F32).astype(jnp.int32)
            zhot[pl.ds(col * 512 + k * 256, 256), :] = jnp.where(
                z == iota((256, 128), 1), 1.0, 0.0
            )

    def arrange(refs, first):
        @pl.loop(0, 32)
        def _(y):
            for j in range(4):
                take = pl.ds(j * 32 + y, 8, stride=128)
                put = pl.multiple_of((first + y) * SLAB + j * 8, 8)
                fld[pl.ds(put + 4 * SLAB, 8), :] = refs[0][take, :]
                fld[pl.ds(put + 4 * SLAB + FIELD, 8), :] = refs[1][take, :]
                h, v = refs[2][take, :], refs[3][take, :]
                hc[pl.ds(put, 8), :] = h
                vc[pl.ds(put, 8), :] = v * (1.0 / SCALE)
                kc[pl.ds(put, 8), :] = 2.0 + COEF[0] * (2.0 * h + v)

    arrange((p_ref, q_ref, h_ref, v_ref), 32 * half)
    raw[0] = decode(oh_ref[...])
    raw[1] = decode(ov_ref[...])
    arrange((op_ref, oq_ref, raw.at[0], raw.at[1]), 32 - 32 * half)

    sub, lane = iota((8, 128), 0), iota((8, 128), 1)
    group = lax.rem((lane + 4) // 8, 16)
    rim = (lane < 4) | (lane >= 124)
    lower = lax.rem(lane, 8) < 4

    def y_copy(side, par):
        src = par * FIELD + (4 if side == 0 else NY) * SLAB
        dst = par * FIELD + (NY + 4 if side == 0 else 0) * SLAB
        return pltpu.make_async_remote_copy(
            src_ref=fld.at[pl.ds(pl.multiple_of(src, 128), 128)],
            dst_ref=fld.at[pl.ds(pl.multiple_of(dst, 128), 128)],
            send_sem=ysend.at[side],
            recv_sem=yrecv.at[1 - side, par],
            device_id=peer["y", side],
            device_id_type=MESH,
        )

    def y_wait(side, par):
        here = pl.ds(pl.multiple_of(par * FIELD + (0 if side == 0 else NY + 4) * SLAB, 128), 128)
        pltpu.make_async_remote_copy(
            src_ref=fld.at[here], dst_ref=fld.at[here], send_sem=ysend.at[side],
            recv_sem=yrecv.at[side, par], device_id=peer["y", side], device_id_type=MESH,
        ).wait_recv()

    def x_copy(side, c, par, there):
        rows = pl.ds(pl.multiple_of(c * CHUNK * 4, 64), CHUNK * 4)
        return pltpu.make_async_remote_copy(
            src_ref=xs.at[side, rows],
            dst_ref=xh.at[par, there, rows],
            send_sem=xsend.at[side, c],
            recv_sem=xrecv.at[there, par, c],
            device_id=peer["x", side],
            device_id_type=MESH,
        )

    def z_copy(side, c, par, there):
        return pltpu.make_async_remote_copy(
            src_ref=zs.at[c],
            dst_ref=zh.at[par, c, there],
            send_sem=zsend.at[side, c],
            recv_sem=zrecv.at[there, par, c],
            device_id=peer["z", side],
            device_id_type=MESH,
        )

    def settle(c):
        for side in range(2):

            @pl.when(has["x", side])
            def _():
                x_copy(side, c, 0, 1 - side).wait_send()

            @pl.when(has["z", side])
            def _():
                z_copy(side, c, 0, 1 - side).wait_send()

            @pl.when(has["y", side] & (c == (0 if side == 0 else NCH - 1)))
            def _():
                y_copy(side, 0).wait_send()

    def send(c, par):
        for side in range(2):

            @pl.when(has["y", side] & (c == (0 if side == 0 else NCH - 1)))
            def _():
                y_copy(side, par).start()

        first = par * FIELD + (4 + c * CHUNK) * SLAB
        rows = pl.ds(pl.multiple_of(c * CHUNK * 4, 64), CHUNK * 4)
        for side in range(2):
            xs[side, rows, :] = fld[pl.ds(first + 7 * side, CHUNK * 4, stride=8), :]

            @pl.when(has["x", side])
            def _():
                x_copy(side, c, par, 1 - side).start()

        start = pl.multiple_of(c * ROWS, ROWS)
        both = jnp.dot(hl[pl.ds(start, ROWS), :], band[...], preferred_element_type=F32)
        lap[pl.ds(start, ROWS), :] = both[:, 0:128]
        for n in range(4):
            packed = both[128 * n : 128 * n + 8, 128:256]
            for i in range(1, 16):
                at = 128 * n + 8 * i
                packed = jnp.where(group == i, both[at : at + 8, 128:256], packed)
            zs[c, pl.ds(8 * n, 8), :] = packed
        for side in range(2):

            @pl.when(has["z", side])
            def _():
                z_copy(side, c, par, 1 - side).start()

    def split(start, new):
        high = new.astype(BF16)
        hl[pl.ds(start, SLAB), 0:128] = high
        hl[pl.ds(start, SLAB), 128:256] = (new - high.astype(F32)).astype(BF16)

    @pl.loop(0, NCH)
    def _(i):
        c = jnp.where(i == 0, 0, jnp.where(i == 1, NCH - 1, i - 1))

        @pl.loop(0, CHUNK)
        def _(y):
            start = pl.multiple_of(c * ROWS + y * SLAB, SLAB)
            split(start, fld[pl.ds(start + 4 * SLAB, SLAB), :])

        send(c, 0)

    def step(t, carry):
        par = lax.rem(t, 2)
        old, now = (1 - par) * FIELD + 4 * SLAB, par * FIELD + 4 * SLAB

        @pl.when(par == 0)
        def _():
            for col in range(2):
                for k in range(2):
                    when = 64 * k + t + iota((128, 256), 1) // 128
                    spread = jnp.where(iota((128, 256), 0) == when, 1.0, 0.0).astype(BF16)
                    amp = jnp.dot(f_ref[col], spread, preferred_element_type=F32)
                    at = pl.ds(col * 512 + k * 256, 256)
                    wgt[at, 0:128] = (zhot[at, :] * amp[:, 0:128]).astype(BF16)
                    wgt[at, 128:256] = (zhot[at, :] * amp[:, 128:256]).astype(BF16)

            @pl.loop(0, 2 * NCH)
            def _(b):
                rows = pl.ds(pl.multiple_of(b * 256, 256), 256)
                col = pl.multiple_of((b // NCH) * 512, 512)
                both = jnp.dot(
                    hot[rows, :], wgt[pl.ds(col, 512), :], preferred_element_type=F32
                )
                src[0, rows, :] = both[:, 0:128]
                src[1, rows, :] = both[:, 128:256]

        @pl.loop(0, NCH)
        def _(i):
            c = jnp.where(i == 0, 0, jnp.where(i == 1, NCH - 1, i - 1))
            first = pl.multiple_of(c * ROWS, ROWS)
            for side in range(2):

                @pl.when(has["y", side] & (c == (0 if side == 0 else NCH - 1)))
                def _():
                    y_wait(side, par)

                @pl.when(has["x", side])
                def _():
                    x_copy(side, c, par, side).wait_recv()
                    rows = pl.ds(pl.multiple_of(c * CHUNK * 4, 64), CHUNK * 4)
                    hb[pl.ds(first + 7 * side, CHUNK * 4, stride=8), :] = xh[par, side, rows, :]

                @pl.when(has["z", side])
                def _():
                    z_copy(side, c, par, side).wait_recv()

            settle(c)

            @pl.loop(0, CHUNK // GROUP)
            def _(y):
                at = pl.multiple_of(y * (GROUP * SLAB), GROUP * SLAB)
                r = pl.multiple_of(first + at, GROUP * SLAB)
                base = pl.multiple_of(now + r, SLAB)
                back = pl.multiple_of(old + r, SLAB)
                mine = pl.ds(pl.multiple_of(y * 8, 8), 8)
                got = jnp.where(lower, zh[par, c, 0, mine, :], zh[par, c, 1, mine, :])
                fresh = []
                for g in range(GROUP):
                    mid = [fld[pl.ds(base + SLAB * g + 8 * j, 8), :] for j in range(4)]
                    edge = [hb[pl.ds(r + SLAB * g + 8 * j, 8), :] for j in range(4)]
                    below = [jnp.where(sub == 0, e, pltpu.roll(v, 1, 0)) for e, v in zip(edge, mid)]
                    above = [jnp.where(sub == 7, e, pltpu.roll(v, 7, 0)) for e, v in zip(edge, mid)]
                    line = below + mid + above
                    tiles = []
                    for j in range(4):
                        spot = SLAB * g + 8 * j
                        total = None
                        for k in range(1, 5):
                            near = (line[4 + j + k] + line[4 + j - k]) + (
                                fld[pl.ds(base + spot + k * SLAB, 8), :]
                                + fld[pl.ds(base + spot - k * SLAB, 8), :]
                            )
                            near = COEF[k] * near
                            total = near if total is None else total + near
                        here = pl.ds(r + spot, 8)
                        turn = (128 - spot) % 128
                        rolled = pltpu.roll(got, turn, 1) if turn else got
                        depth = lap[here, :] + jnp.where(rim, rolled, 0.0)
                        tiles.append(
                            (src[par, here, :] - fld[pl.ds(back + spot, 8), :])
                            + kc[here, :] * mid[j]
                            + hc[here, :] * total
                            + vc[here, :] * depth
                        )
                    fresh.append(jnp.concatenate(tiles, axis=0))
                for g, new in enumerate(fresh):
                    fld[pl.ds(back + SLAB * g, SLAB), :] = new
                    split(pl.multiple_of(r + SLAB * g, SLAB), new)

            @pl.when(t < STEPS - 1)
            def _():
                send(c, 1 - par)

        return carry

    lax.fori_loop(0, STEPS, step, 0)
    @pl.loop(0, 32)
    def _(y):
        for j in range(4):
            put = pl.ds(j * 32 + y, 8, stride=128)
            take = pl.multiple_of((4 + 32 * half + y) * SLAB + j * 8, 8)
            outp_ref[put, :] = fld[pl.ds(take, 8), :]
            outq_ref[put, :] = fld[pl.ds(take + FIELD, 8), :]


def body(
    pressure, pressure_prev, horiz_coef, vert_coef, traces, recv_cell, recv_owner, trace_counts
):
    pairs = [(i, i ^ 1) for i in range(lax.axis_size("gy"))]

    def swap(array):
        return lax.ppermute(array, "gy", pairs)

    blocks = [a.reshape(1024, 128) for a in (pressure, pressure_prev, horiz_coef, vert_coef)]
    blocks += [swap(a) for a in (blocks[0], blocks[1], code(blocks[2]), code(blocks[3]))]

    samples = traces.shape[-1]
    columns, slots = recv_cell.shape[1:]
    per_step = samples // STEPS
    box_table = (
        jnp.arange(samples, dtype=jnp.int32)[:, None] // per_step
        == STEPS - 1 - jnp.arange(STEPS, dtype=jnp.int32)[None, :]
    ).astype(BF16)
    amps = jnp.dot(
        traces.reshape(-1, samples), box_table, preferred_element_type=F32
    ).astype(BF16).reshape(columns, slots, STEPS)
    cell = recv_cell[0]
    x, y, z = cell // 4096, (cell // 128) % 32, cell % 128
    live = jnp.arange(slots, dtype=jnp.int32)[None, :] < trace_counts[0][:, None]
    owner = jnp.where(live, recv_owner[0], -1)
    tags = jnp.stack([y, (x % 4) * 8 + x // 4, z, owner], axis=-1).astype(BF16)
    packed = jnp.concatenate(
        [amps, tags, jnp.zeros((columns, slots, 28), BF16)], axis=-1
    ).reshape(columns, 128)
    routed = lax.all_to_all(packed, ("gx", "gy"), split_axis=0, concat_axis=0, tiled=True)
    own = lax.all_gather(routed, "gz", axis=0, tiled=True)
    other = swap(own)
    low = lax.rem(lax.axis_index("gy"), 2) == 0
    table = jnp.stack([jnp.where(low, own, other), jnp.where(low, other, own)])

    vmem = pl.BlockSpec(memory_space=pltpu.VMEM)
    dma = pltpu.SemaphoreType.DMA
    outs = pl.pallas_call(
        kernel,
        out_shape=[jax.ShapeDtypeStruct((1024, 128), F32)] * 2,
        in_specs=[vmem] * 9,
        out_specs=[vmem] * 2,
        scratch_shapes=[
            pltpu.VMEM((2 * FIELD, 128), F32),
            pltpu.VMEM((NY * SLAB, 128), F32),
            pltpu.VMEM((NY * SLAB, 128), F32),
            pltpu.VMEM((NY * SLAB, 128), F32),
            pltpu.VMEM((NY * SLAB, 256), BF16),
            pltpu.VMEM((NY * SLAB, 512), BF16),
            pltpu.VMEM((1024, 128), F32),
            pltpu.VMEM((1024, 256), BF16),
            pltpu.VMEM((2, NY * 4, 128), F32),
            pltpu.VMEM((2, 2, NY * 4, 128), F32),
            pltpu.VMEM((NY * SLAB, 128), F32),
            pltpu.VMEM((NCH, 32, 128), F32),
            pltpu.VMEM((2, NCH, 2, 32, 128), F32),
            pltpu.VMEM((2, 1024, 128), F32),
            pltpu.VMEM((256, 256), BF16),
            pltpu.VMEM((NY * SLAB, 128), F32),
            pltpu.VMEM((2, NY * SLAB, 128), F32),
            dma((2,)), dma((2, 2)),
            dma((2, NCH)), dma((2, 2, NCH)),
            dma((2, NCH)), dma((2, 2, NCH)),
        ],
        compiler_params=pltpu.CompilerParams(
            collective_id=0, has_side_effects=True, vmem_limit_bytes=40 * 1024 * 1024
        ),
    )(*blocks, table)
    return tuple(o.reshape(32, 32, 128) for o in outs)


def solution(mesh):
    block = P("gx", "gy", "gz")
    placed = (
        block,
        block,
        block,
        block,
        P(("gx", "gy", "gz"), None, None, None),
        P(("gx", "gy", "gz"), None, None),
        P(("gx", "gy", "gz"), None, None),
        P(("gx", "gy", "gz"), None),
    )
    return jax.shard_map(
        body, mesh=mesh, in_specs=placed, out_specs=(block, block), check_vma=False
    )
```

```python
import functools

import jax
import jax.numpy as jnp
from jax import lax
from jax.experimental import pallas as pl
from jax.experimental.pallas import tpu as pltpu
from jax.sharding import PartitionSpec as P

STEPS = 32
MESH = pl.DeviceIdType.MESH
COEF = (-205.0 / 72.0, 8.0 / 5.0, -1.0 / 5.0, 8.0 / 315.0, -1.0 / 560.0)
SCALE = 5040.0
TAPS = (8064.0, -1008.0, 128.0, -9.0)

NY = 64
CHUNK = 16
NCH = NY // CHUNK
ROWS = CHUNK * 32
GROUP = 4
SLAB = 32
FIELD = (NY + 8) * SLAB
F32, BF16 = jnp.float32, jnp.bfloat16


def taps(distance):
    value = jnp.zeros(distance.shape, F32)
    for k in range(1, 5):
        value = jnp.where(distance == k, TAPS[k - 1], value)
    return value


def code(value):
    return jnp.round((value - 0.115) * (32767.0 / 0.075)).astype(jnp.int32).astype(jnp.int16)


def decode(value):
    return value.astype(jnp.int32).astype(F32) * (0.075 / 32767.0) + 0.115


def iota(shape, dim):
    return lax.broadcasted_iota(jnp.int32, shape, dim)


def kernel(
    p_ref, q_ref, h_ref, v_ref, f_ref, outp_ref, outq_ref,
    fld, hc, vc, kc, hl, hot, zhot, wgt, xs, xh, hb, zs, zh, raw, coded, rawcoded, peak, rawpeak, table, band, lap, src,
    ysend, yrecv, xsend, xrecv, zsend, zrecv, psend, precv, tsend, trecv,
):
    gx, gy, gz = lax.axis_index("gx"), lax.axis_index("gy"), lax.axis_index("gz")
    nx, ny, nz = lax.axis_size("gx"), lax.axis_size("gy"), lax.axis_size("gz")
    half = lax.rem(gy, 2)
    partner = gy + 1 - 2 * half
    flip = lax.rem(gy // 2, 2) * (NCH - 1)
    has = {
        ("x", 0): gx > 0, ("x", 1): gx < nx - 1,
        ("y", 0): gy > 1, ("y", 1): gy < ny - 2,
        ("z", 0): gz > 0, ("z", 1): gz < nz - 1,
    }
    peer = {
        ("x", 0): {"gx": gx - 1}, ("x", 1): {"gx": gx + 1},
        ("y", 0): {"gy": gy - 2}, ("y", 1): {"gy": gy + 2},
        ("z", 0): {"gz": gz - 1}, ("z", 1): {"gz": gz + 1},
    }

    def clear(ref, start, count):
        ref[pl.ds(start, count), :] = jnp.zeros((count, 128), F32)

    for par in range(2):
        clear(fld, par * FIELD, 4 * SLAB)
        clear(fld, par * FIELD + (NY + 4) * SLAB, 4 * SLAB)
    zh[...] = jnp.zeros_like(zh)

    mates = [
        (n, {"gy": gy if same else partner, "gz": lax.rem(gz + d, nz)})
        for n, (same, d) in enumerate([(s, d) for s in (True, False) for d in range(nz)][1:])
    ]
    barrier = pltpu.get_barrier_semaphore()
    for _, mate in mates:
        pl.semaphore_signal(barrier, inc=1, device_id=mate, device_id_type=MESH)
    greet = jnp.int32(len(mates))
    for key, ok in has.items():

        @pl.when(ok)
        def _(key=key):
            pl.semaphore_signal(barrier, inc=1, device_id=peer[key], device_id_type=MESH)

        greet = greet + ok.astype(jnp.int32)
    pl.semaphore_wait(barrier, greet)

    def tell(n, mate, col, depth):
        return pltpu.make_async_remote_copy(
            src_ref=f_ref,
            dst_ref=table.at[col, depth],
            send_sem=tsend.at[n],
            recv_sem=trecv.at[col, depth],
            device_id=mate,
            device_id_type=MESH,
        )

    for n, mate in mates:
        tell(n, mate, half, gz).start()
    table[half, gz] = f_ref[...]

    def pair(n):
        src_ref = coded.at[n] if n < 4 else peak
        dst_ref = rawcoded.at[n] if n < 4 else rawpeak
        return pltpu.make_async_remote_copy(
            src_ref=src_ref,
            dst_ref=dst_ref,
            send_sem=psend.at[n],
            recv_sem=precv.at[n],
            device_id={"gy": partner},
            device_id_type=MESH,
        )

    for n, ref in ((2, h_ref), (3, v_ref)):
        coded[n] = code(ref[...])
    for n, ref in ((0, p_ref), (1, q_ref)):

        @pl.loop(0, 32)
        def _(x):
            rows = pl.ds(pl.multiple_of(x * 32, 32), 32)
            value = ref[rows, :]
            top = jnp.max(jnp.abs(value), axis=0, keepdims=True)
            top = jnp.where(top > 0.0, top, 1.0)
            peak[n, pl.ds(x, 1), :] = top
            coded[n, rows, :] = jnp.round(value / top * 32767.0).astype(jnp.int32).astype(jnp.int16)

    for n, (same, d) in enumerate([(s, d) for s in (True, False) for d in range(nz)][1:]):
        col, depth = half if same else 1 - half, lax.rem(gz + d, nz)
        tell(n, mates[n][1], col, depth).wait_recv()
    for n in range(5):
        pair(n).start()

    @pl.loop(0, NCH)
    def _(c):
        clear(hb, pl.multiple_of(c * ROWS, ROWS), ROWS)

    depth = lax.rem(iota((256, 128), 0), 128)
    band[:, 0:128] = taps(jnp.abs(depth - iota((256, 128), 1))).astype(BF16)
    m = lax.rem(iota((256, 128), 1), 8)
    band[:, 128:256] = taps(jnp.where(m < 4, 128 + m - depth, depth + 8 - m)).astype(BF16)

    for col in range(2):
        packed = table[col].reshape(256, 128)
        for k in range(2):
            pick = iota((8, 128), 1) == 64 * k + 32 + iota((8, 128), 0)
            by_lane = lax.dot_general(
                jnp.where(pick, 1.0, 0.0).astype(BF16), packed,
                (((1,), (1,)), ((), ())), preferred_element_type=F32,
            )
            where = (by_lane[0:1] * 32.0 + by_lane[1:2]).astype(jnp.int32)
            mine = by_lane[3:4].astype(jnp.int32) == gz
            where = jnp.where(mine, where, -1)
            for block in range(4):
                at = iota((256, 256), 0) + block * 256
                hot[pl.ds(col * 1024 + block * 256, 256), pl.ds(k * 256, 256)] = jnp.where(
                    at == where, 1.0, 0.0
                ).astype(BF16)
            spread = jnp.where(iota((128, 128), 0) == 64 * k + 34, 1.0, 0.0).astype(BF16)
            z = jnp.dot(packed, spread, preferred_element_type=F32).astype(jnp.int32)
            zhot[pl.ds(col * 512 + k * 256, 256), :] = jnp.where(
                z == iota((256, 128), 1), 1.0, 0.0
            )

    def arrange(refs, first):
        @pl.loop(0, 32)
        def _(y):
            for j in range(4):
                take = pl.ds(j * 32 + y, 8, stride=128)
                put = pl.multiple_of((first + y) * SLAB + j * 8, 8)
                fld[pl.ds(put + 4 * SLAB, 8), :] = refs[0][take, :]
                fld[pl.ds(put + 4 * SLAB + FIELD, 8), :] = refs[1][take, :]
                h, v = refs[2][take, :], refs[3][take, :]
                hc[pl.ds(put, 8), :] = h
                vc[pl.ds(put, 8), :] = v * (1.0 / SCALE)
                kc[pl.ds(put, 8), :] = 2.0 + COEF[0] * (2.0 * h + v)

    arrange((p_ref, q_ref, h_ref, v_ref), 32 * half)
    @pl.loop(0, STEPS // 2)
    def _(u):
        for col in range(2):
            for k in range(2):
                when = 64 * k + 2 * u + iota((128, 256), 1) // 128
                spread = jnp.where(iota((128, 256), 0) == when, 1.0, 0.0).astype(BF16)
                amp = jnp.dot(table[col].reshape(256, 128), spread, preferred_element_type=F32)
                at = pl.ds(col * 512 + k * 256, 256)
                wgt[at, 0:128] = (zhot[at, :] * amp[:, 0:128]).astype(BF16)
                wgt[at, 128:256] = (zhot[at, :] * amp[:, 128:256]).astype(BF16)

        @pl.loop(0, 2 * NCH)
        def _(b):
            rows = pl.ds(pl.multiple_of(b * 256, 256), 256)
            col = pl.multiple_of((b // NCH) * 512, 512)
            both = jnp.dot(hot[rows, :], wgt[pl.ds(col, 512), :], preferred_element_type=F32)
            src[2 * u, rows, :] = both[:, 0:128]
            src[2 * u + 1, rows, :] = both[:, 128:256]

    for n in range(5):
        pair(n).wait_recv()
    for n in range(2):
        raw[2 + n] = decode(rawcoded[2 + n])

        @pl.loop(0, 32)
        def _(x):
            rows = pl.ds(pl.multiple_of(x * 32, 32), 32)
            scale = rawpeak[n, pl.ds(x, 1), :] * (1.0 / 32767.0)
            raw[n, rows, :] = rawcoded[n, rows, :].astype(jnp.int32).astype(F32) * scale

    arrange([raw.at[n] for n in range(4)], 32 - 32 * half)

    sub, lane = iota((8, 128), 0), iota((8, 128), 1)
    group = lax.rem((lane + 4) // 8, 16)
    rim = (lane < 4) | (lane >= 124)
    lower = lax.rem(lane, 8) < 4

    def y_copy(side, par):
        src = par * FIELD + (4 if side == 0 else NY) * SLAB
        dst = par * FIELD + (NY + 4 if side == 0 else 0) * SLAB
        return pltpu.make_async_remote_copy(
            src_ref=fld.at[pl.ds(pl.multiple_of(src, 128), 128)],
            dst_ref=fld.at[pl.ds(pl.multiple_of(dst, 128), 128)],
            send_sem=ysend.at[side],
            recv_sem=yrecv.at[1 - side, par],
            device_id=peer["y", side],
            device_id_type=MESH,
        )

    def y_wait(side, par):
        here = pl.ds(pl.multiple_of(par * FIELD + (0 if side == 0 else NY + 4) * SLAB, 128), 128)
        pltpu.make_async_remote_copy(
            src_ref=fld.at[here], dst_ref=fld.at[here], send_sem=ysend.at[side],
            recv_sem=yrecv.at[side, par], device_id=peer["y", side], device_id_type=MESH,
        ).wait_recv()

    def x_copy(side, c, par, there):
        rows = pl.ds(pl.multiple_of(c * CHUNK * 4, 64), CHUNK * 4)
        return pltpu.make_async_remote_copy(
            src_ref=xs.at[side, rows],
            dst_ref=xh.at[par, there, rows],
            send_sem=xsend.at[side, c],
            recv_sem=xrecv.at[there, par, c],
            device_id=peer["x", side],
            device_id_type=MESH,
        )

    def z_copy(side, c, par, there):
        return pltpu.make_async_remote_copy(
            src_ref=zs.at[c],
            dst_ref=zh.at[par, c, there],
            send_sem=zsend.at[side, c],
            recv_sem=zrecv.at[there, par, c],
            device_id=peer["z", side],
            device_id_type=MESH,
        )

    def settle(c):
        for side in range(2):

            @pl.when(has["x", side])
            def _():
                x_copy(side, c, 0, 1 - side).wait_send()

            @pl.when(has["z", side])
            def _():
                z_copy(side, c, 0, 1 - side).wait_send()

            @pl.when(has["y", side] & (c == (0 if side == 0 else NCH - 1)))
            def _():
                y_copy(side, 0).wait_send()

    def send(c, par):
        for side in range(2):

            @pl.when(has["y", side] & (c == (0 if side == 0 else NCH - 1)))
            def _():
                y_copy(side, par).start()

        first = par * FIELD + (4 + c * CHUNK) * SLAB
        rows = pl.ds(pl.multiple_of(c * CHUNK * 4, 64), CHUNK * 4)
        for side in range(2):
            xs[side, rows, :] = fld[pl.ds(first + 7 * side, CHUNK * 4, stride=8), :]

            @pl.when(has["x", side])
            def _():
                x_copy(side, c, par, 1 - side).start()

        start = pl.multiple_of(c * ROWS, ROWS)
        both = jnp.dot(hl[pl.ds(start, ROWS), :], band[...], preferred_element_type=F32)
        lap[pl.ds(start, ROWS), :] = both[:, 0:128]
        for n in range(4):
            packed = both[128 * n : 128 * n + 8, 128:256]
            for i in range(1, 16):
                at = 128 * n + 8 * i
                packed = jnp.where(group == i, both[at : at + 8, 128:256], packed)
            zs[c, pl.ds(8 * n, 8), :] = packed
        for side in range(2):

            @pl.when(has["z", side])
            def _():
                z_copy(side, c, par, 1 - side).start()

    def split(start, new):
        high = new.astype(BF16)
        hl[pl.ds(start, SLAB), 0:128] = high
        hl[pl.ds(start, SLAB), 128:256] = (new - high.astype(F32)).astype(BF16)

    @pl.loop(0, NCH)
    def _(i):
        c = jnp.where(i == 0, flip, jnp.where(i == 1, NCH - 1 - flip, i - 1))

        @pl.loop(0, CHUNK)
        def _(y):
            start = pl.multiple_of(c * ROWS + y * SLAB, SLAB)
            split(start, fld[pl.ds(start + 4 * SLAB, SLAB), :])

        send(c, 0)

    def step(t, carry):
        par = lax.rem(t, 2)
        old, now = (1 - par) * FIELD + 4 * SLAB, par * FIELD + 4 * SLAB

        @pl.loop(0, NCH)
        def _(i):
            c = jnp.where(i == 0, flip, jnp.where(i == 1, NCH - 1 - flip, i - 1))
            first = pl.multiple_of(c * ROWS, ROWS)
            for side in range(2):

                @pl.when(has["y", side] & (c == (0 if side == 0 else NCH - 1)))
                def _():
                    y_wait(side, par)

                @pl.when(has["x", side])
                def _():
                    x_copy(side, c, par, side).wait_recv()
                    rows = pl.ds(pl.multiple_of(c * CHUNK * 4, 64), CHUNK * 4)
                    hb[pl.ds(first + 7 * side, CHUNK * 4, stride=8), :] = xh[par, side, rows, :]

                @pl.when(has["z", side])
                def _():
                    z_copy(side, c, par, side).wait_recv()

            settle(c)

            @pl.loop(0, CHUNK // GROUP)
            def _(y):
                at = pl.multiple_of(y * (GROUP * SLAB), GROUP * SLAB)
                r = pl.multiple_of(first + at, GROUP * SLAB)
                base = pl.multiple_of(now + r, SLAB)
                back = pl.multiple_of(old + r, SLAB)
                mine = pl.ds(pl.multiple_of(y * 8, 8), 8)
                got = jnp.where(lower, zh[par, c, 0, mine, :], zh[par, c, 1, mine, :])
                fresh = []
                for g in range(GROUP):
                    mid = [fld[pl.ds(base + SLAB * g + 8 * j, 8), :] for j in range(4)]
                    edge = [hb[pl.ds(r + SLAB * g + 8 * j, 8), :] for j in range(4)]
                    below = [jnp.where(sub == 0, e, pltpu.roll(v, 1, 0)) for e, v in zip(edge, mid)]
                    above = [jnp.where(sub == 7, e, pltpu.roll(v, 7, 0)) for e, v in zip(edge, mid)]
                    line = below + mid + above
                    tiles = []
                    for j in range(4):
                        spot = SLAB * g + 8 * j
                        total = None
                        for k in range(1, 5):
                            near = (line[4 + j + k] + line[4 + j - k]) + (
                                fld[pl.ds(base + spot + k * SLAB, 8), :]
                                + fld[pl.ds(base + spot - k * SLAB, 8), :]
                            )
                            near = COEF[k] * near
                            total = near if total is None else total + near
                        here = pl.ds(r + spot, 8)
                        turn = (128 - spot) % 128
                        rolled = pltpu.roll(got, turn, 1) if turn else got
                        depth = lap[here, :] + jnp.where(rim, rolled, 0.0)
                        tiles.append(
                            (src[t, here, :] - fld[pl.ds(back + spot, 8), :])
                            + kc[here, :] * mid[j]
                            + hc[here, :] * total
                            + vc[here, :] * depth
                        )
                    fresh.append(jnp.concatenate(tiles, axis=0))
                for g, new in enumerate(fresh):
                    fld[pl.ds(back + SLAB * g, SLAB), :] = new
                    split(pl.multiple_of(r + SLAB * g, SLAB), new)

            @pl.when(t < STEPS - 1)
            def _():
                send(c, 1 - par)

        return carry

    lax.fori_loop(0, STEPS, step, 0)
    for n in range(5):
        pair(n).wait_send()
    for n, mate in mates:
        tell(n, mate, half, gz).wait_send()
    @pl.loop(0, 32)
    def _(y):
        for j in range(4):
            put = pl.ds(j * 32 + y, 8, stride=128)
            take = pl.multiple_of((4 + 32 * half + y) * SLAB + j * 8, 8)
            outp_ref[put, :] = fld[pl.ds(take, 8), :]
            outq_ref[put, :] = fld[pl.ds(take + FIELD, 8), :]


def body(
    pressure, pressure_prev, horiz_coef, vert_coef, traces, recv_cell, recv_owner, trace_counts
):
    blocks = [a.reshape(1024, 128) for a in (pressure, pressure_prev, horiz_coef, vert_coef)]

    samples = traces.shape[-1]
    columns, slots = recv_cell.shape[1:]
    per_step = samples // STEPS
    box_table = (
        jnp.arange(samples, dtype=jnp.int32)[:, None] // per_step
        == STEPS - 1 - jnp.arange(STEPS, dtype=jnp.int32)[None, :]
    ).astype(BF16)
    amps = jnp.dot(
        traces.reshape(-1, samples), box_table, preferred_element_type=F32
    ).astype(BF16).reshape(columns, slots, STEPS)
    cell = recv_cell[0]
    x, y, z = cell // 4096, (cell // 128) % 32, cell % 128
    live = jnp.arange(slots, dtype=jnp.int32)[None, :] < trace_counts[0][:, None]
    owner = jnp.where(live, recv_owner[0], -1)
    tags = jnp.stack([y, (x % 4) * 8 + x // 4, z, owner], axis=-1).astype(BF16)
    packed = jnp.concatenate(
        [amps, tags, jnp.zeros((columns, slots, 28), BF16)], axis=-1
    ).reshape(columns, 128)
    routed = lax.all_to_all(packed, ("gx", "gy"), split_axis=0, concat_axis=0, tiled=True)

    vmem = pl.BlockSpec(memory_space=pltpu.VMEM)
    dma = pltpu.SemaphoreType.DMA
    outs = pl.pallas_call(
        kernel,
        out_shape=[jax.ShapeDtypeStruct((1024, 128), F32)] * 2,
        in_specs=[vmem] * 5,
        out_specs=[vmem] * 2,
        scratch_shapes=[
            pltpu.VMEM((2 * FIELD, 128), F32),
            pltpu.VMEM((NY * SLAB, 128), F32),
            pltpu.VMEM((NY * SLAB, 128), F32),
            pltpu.VMEM((NY * SLAB, 128), F32),
            pltpu.VMEM((NY * SLAB, 256), BF16),
            pltpu.VMEM((NY * SLAB, 512), BF16),
            pltpu.VMEM((1024, 128), F32),
            pltpu.VMEM((1024, 256), BF16),
            pltpu.VMEM((2, NY * 4, 128), F32),
            pltpu.VMEM((2, 2, NY * 4, 128), F32),
            pltpu.VMEM((NY * SLAB, 128), F32),
            pltpu.VMEM((NCH, 32, 128), F32),
            pltpu.VMEM((2, NCH, 2, 32, 128), F32),
            pltpu.VMEM((4, 1024, 128), F32),
            pltpu.VMEM((4, 1024, 128), jnp.int16),
            pltpu.VMEM((4, 1024, 128), jnp.int16),
            pltpu.VMEM((2, 32, 128), F32),
            pltpu.VMEM((2, 32, 128), F32),
            pltpu.VMEM((2, 4, 64, 128), BF16),
            pltpu.VMEM((256, 256), BF16),
            pltpu.VMEM((NY * SLAB, 128), F32),
            pltpu.VMEM((STEPS, NY * SLAB, 128), F32),
            dma((2,)), dma((2, 2)),
            dma((2, NCH)), dma((2, 2, NCH)),
            dma((2, NCH)), dma((2, 2, NCH)),
            dma((5,)), dma((5,)),
            dma((7,)), dma((2, 4)),
        ],
        compiler_params=pltpu.CompilerParams(
            collective_id=0, has_side_effects=True, vmem_limit_bytes=54 * 1024 * 1024
        ),
    )(*blocks, routed)
    return tuple(o.reshape(32, 32, 128) for o in outs)


def solution(mesh):
    block = P("gx", "gy", "gz")
    placed = (
        block,
        block,
        block,
        block,
        P(("gx", "gy", "gz"), None, None, None),
        P(("gx", "gy", "gz"), None, None),
        P(("gx", "gy", "gz"), None, None),
        P(("gx", "gy", "gz"), None),
    )
    return jax.shard_map(
        body, mesh=mesh, in_specs=placed, out_specs=(block, block), check_vma=False
    )
```

```python
import functools

import jax
import jax.numpy as jnp
from jax import lax
from jax.experimental import pallas as pl
from jax.experimental.pallas import tpu as pltpu
from jax.sharding import PartitionSpec as P

STEPS = 32
MESH = pl.DeviceIdType.MESH
COEF = (-205.0 / 72.0, 8.0 / 5.0, -1.0 / 5.0, 8.0 / 315.0, -1.0 / 560.0)
SCALE = 5040.0
TAPS = (8064.0, -1008.0, 128.0, -9.0)

NY = 64
CHUNK = 16
NCH = NY // CHUNK
ROWS = CHUNK * 32
GROUP = 4
SLAB = 32
FIELD = (NY + 8) * SLAB
F32, BF16 = jnp.float32, jnp.bfloat16


def taps(distance):
    value = jnp.zeros(distance.shape, F32)
    for k in range(1, 5):
        value = jnp.where(distance == k, TAPS[k - 1], value)
    return value


def code(value):
    return jnp.round((value - 0.115) * (32767.0 / 0.075)).astype(jnp.int32).astype(jnp.int16)


def decode(value):
    return value.astype(jnp.int32).astype(F32) * (0.075 / 32767.0) + 0.115


def iota(shape, dim):
    return lax.broadcasted_iota(jnp.int32, shape, dim)


def kernel(
    p_ref, q_ref, h_ref, v_ref, rawcoded, rawpeak, f_ref, outp_ref, outq_ref,
    fld, hc, vc, kc, hl, hot, zhot, wgt, xs, xh, hb, zs, zh, raw, table, band, lap, src,
    ysend, yrecv, xsend, xrecv, zsend, zrecv, tsend, trecv,
):
    gx, gy, gz = lax.axis_index("gx"), lax.axis_index("gy"), lax.axis_index("gz")
    nx, ny, nz = lax.axis_size("gx"), lax.axis_size("gy"), lax.axis_size("gz")
    half = lax.rem(gy, 2)
    partner = gy + 1 - 2 * half
    flip = lax.rem(gy // 2, 2) * (NCH - 1)
    has = {
        ("x", 0): gx > 0, ("x", 1): gx < nx - 1,
        ("y", 0): gy > 1, ("y", 1): gy < ny - 2,
        ("z", 0): gz > 0, ("z", 1): gz < nz - 1,
    }
    peer = {
        ("x", 0): {"gx": gx - 1}, ("x", 1): {"gx": gx + 1},
        ("y", 0): {"gy": gy - 2}, ("y", 1): {"gy": gy + 2},
        ("z", 0): {"gz": gz - 1}, ("z", 1): {"gz": gz + 1},
    }

    def clear(ref, start, count):
        ref[pl.ds(start, count), :] = jnp.zeros((count, 128), F32)

    for par in range(2):
        clear(fld, par * FIELD, 4 * SLAB)
        clear(fld, par * FIELD + (NY + 4) * SLAB, 4 * SLAB)
    zh[...] = jnp.zeros_like(zh)

    mates = [
        (n, {"gy": gy if same else partner, "gz": lax.rem(gz + d, nz)})
        for n, (same, d) in enumerate([(s, d) for s in (True, False) for d in range(nz)][1:])
    ]
    barrier = pltpu.get_barrier_semaphore()
    for _, mate in mates:
        pl.semaphore_signal(barrier, inc=1, device_id=mate, device_id_type=MESH)
    greet = jnp.int32(len(mates))
    for key, ok in has.items():

        @pl.when(ok)
        def _(key=key):
            pl.semaphore_signal(barrier, inc=1, device_id=peer[key], device_id_type=MESH)

        greet = greet + ok.astype(jnp.int32)
    pl.semaphore_wait(barrier, greet)

    def tell(n, mate, col, depth):
        return pltpu.make_async_remote_copy(
            src_ref=f_ref,
            dst_ref=table.at[col, depth],
            send_sem=tsend.at[n],
            recv_sem=trecv.at[col, depth],
            device_id=mate,
            device_id_type=MESH,
        )

    for n, mate in mates:
        tell(n, mate, half, gz).start()
    table[half, gz] = f_ref[...]

    for n, (same, d) in enumerate([(s, d) for s in (True, False) for d in range(nz)][1:]):
        col, depth = half if same else 1 - half, lax.rem(gz + d, nz)
        tell(n, mates[n][1], col, depth).wait_recv()

    @pl.loop(0, NCH)
    def _(c):
        clear(hb, pl.multiple_of(c * ROWS, ROWS), ROWS)

    depth = lax.rem(iota((256, 128), 0), 128)
    band[:, 0:128] = taps(jnp.abs(depth - iota((256, 128), 1))).astype(BF16)
    m = lax.rem(iota((256, 128), 1), 8)
    band[:, 128:256] = taps(jnp.where(m < 4, 128 + m - depth, depth + 8 - m)).astype(BF16)

    for col in range(2):
        packed = table[col].reshape(256, 128)
        for k in range(2):
            pick = iota((8, 128), 1) == 64 * k + 32 + iota((8, 128), 0)
            by_lane = lax.dot_general(
                jnp.where(pick, 1.0, 0.0).astype(BF16), packed,
                (((1,), (1,)), ((), ())), preferred_element_type=F32,
            )
            where = (by_lane[0:1] * 32.0 + by_lane[1:2]).astype(jnp.int32)
            mine = by_lane[3:4].astype(jnp.int32) == gz
            where = jnp.where(mine, where, -1)
            for block in range(4):
                at = iota((256, 256), 0) + block * 256
                hot[pl.ds(col * 1024 + block * 256, 256), pl.ds(k * 256, 256)] = jnp.where(
                    at == where, 1.0, 0.0
                ).astype(BF16)
            spread = jnp.where(iota((128, 128), 0) == 64 * k + 34, 1.0, 0.0).astype(BF16)
            z = jnp.dot(packed, spread, preferred_element_type=F32).astype(jnp.int32)
            zhot[pl.ds(col * 512 + k * 256, 256), :] = jnp.where(
                z == iota((256, 128), 1), 1.0, 0.0
            )

    def arrange(refs, first):
        @pl.loop(0, 32, unroll=4)
        def _(y):
            for j in range(4):
                take = pl.ds(j * 32 + y, 8, stride=128)
                put = pl.multiple_of((first + y) * SLAB + j * 8, 8)
                fld[pl.ds(put + 4 * SLAB, 8), :] = refs[0][take, :]
                fld[pl.ds(put + 4 * SLAB + FIELD, 8), :] = refs[1][take, :]
                h, v = refs[2][take, :], refs[3][take, :]
                hc[pl.ds(put, 8), :] = h
                vc[pl.ds(put, 8), :] = v * (1.0 / SCALE)
                kc[pl.ds(put, 8), :] = 2.0 + COEF[0] * (2.0 * h + v)

    arrange((p_ref, q_ref, h_ref, v_ref), 32 * half)
    def sources(u, col):
        for k in range(2):
            when = 64 * k + 2 * u + iota((128, 256), 1) // 128
            spread = jnp.where(iota((128, 256), 0) == when, 1.0, 0.0).astype(BF16)
            amp = jnp.dot(table[col].reshape(256, 128), spread, preferred_element_type=F32)
            at = pl.ds(pl.multiple_of(col * 512 + k * 256, 256), 256)
            wgt[k * 256 : k * 256 + 256, 0:128] = (zhot[at, :] * amp[:, 0:128]).astype(BF16)
            wgt[k * 256 : k * 256 + 256, 128:256] = (zhot[at, :] * amp[:, 128:256]).astype(BF16)
        slot = 2 * lax.rem(u, 2)

        rows = pl.ds(pl.multiple_of(col * 1024, 1024), 1024)
        both = jnp.dot(hot[rows, :], wgt[...], preferred_element_type=F32)
        src[slot, rows, :] = both[:, 0:128]
        src[slot + 1, rows, :] = both[:, 128:256]

    @pl.loop(0, 2)
    def _(col):
        sources(0, col)

    for n in range(2):
        raw[2 + n] = decode(rawcoded[2 + n])

        @pl.loop(0, 32, unroll=8)
        def _(x):
            rows = pl.ds(pl.multiple_of(x * 32, 32), 32)
            scale = rawpeak[n, pl.ds(x, 1), :] * (1.0 / 32767.0)
            raw[n, rows, :] = rawcoded[n, rows, :].astype(jnp.int32).astype(F32) * scale

    arrange([raw.at[n] for n in range(4)], 32 - 32 * half)

    sub, lane = iota((8, 128), 0), iota((8, 128), 1)
    group = lax.rem((lane + 4) // 8, 16)
    rim = (lane < 4) | (lane >= 124)
    lower = lax.rem(lane, 8) < 4

    def y_copy(side, par):
        src = par * FIELD + (4 if side == 0 else NY) * SLAB
        dst = par * FIELD + (NY + 4 if side == 0 else 0) * SLAB
        return pltpu.make_async_remote_copy(
            src_ref=fld.at[pl.ds(pl.multiple_of(src, 128), 128)],
            dst_ref=fld.at[pl.ds(pl.multiple_of(dst, 128), 128)],
            send_sem=ysend.at[side],
            recv_sem=yrecv.at[1 - side, par],
            device_id=peer["y", side],
            device_id_type=MESH,
        )

    def y_wait(side, par):
        here = pl.ds(pl.multiple_of(par * FIELD + (0 if side == 0 else NY + 4) * SLAB, 128), 128)
        pltpu.make_async_remote_copy(
            src_ref=fld.at[here], dst_ref=fld.at[here], send_sem=ysend.at[side],
            recv_sem=yrecv.at[side, par], device_id=peer["y", side], device_id_type=MESH,
        ).wait_recv()

    def x_copy(side, c, par, there):
        rows = pl.ds(pl.multiple_of(c * CHUNK * 4, 64), CHUNK * 4)
        return pltpu.make_async_remote_copy(
            src_ref=xs.at[side, rows],
            dst_ref=xh.at[par, there, rows],
            send_sem=xsend.at[side, c],
            recv_sem=xrecv.at[there, par, c],
            device_id=peer["x", side],
            device_id_type=MESH,
        )

    def z_copy(side, c, par, there):
        return pltpu.make_async_remote_copy(
            src_ref=zs.at[c],
            dst_ref=zh.at[par, c, there],
            send_sem=zsend.at[side, c],
            recv_sem=zrecv.at[there, par, c],
            device_id=peer["z", side],
            device_id_type=MESH,
        )

    def settle(c):
        for side in range(2):

            @pl.when(has["x", side])
            def _():
                x_copy(side, c, 0, 1 - side).wait_send()

            @pl.when(has["z", side])
            def _():
                z_copy(side, c, 0, 1 - side).wait_send()

            @pl.when(has["y", side] & (c == (0 if side == 0 else NCH - 1)))
            def _():
                y_copy(side, 0).wait_send()

    def send(c, par):
        for side in range(2):

            @pl.when(has["y", side] & (c == (0 if side == 0 else NCH - 1)))
            def _():
                y_copy(side, par).start()

        first = par * FIELD + (4 + c * CHUNK) * SLAB
        rows = pl.ds(pl.multiple_of(c * CHUNK * 4, 64), CHUNK * 4)
        for side in range(2):
            xs[side, rows, :] = fld[pl.ds(first + 7 * side, CHUNK * 4, stride=8), :]

            @pl.when(has["x", side])
            def _():
                x_copy(side, c, par, 1 - side).start()

        start = pl.multiple_of(c * ROWS, ROWS)
        both = jnp.dot(hl[pl.ds(start, ROWS), :], band[...], preferred_element_type=F32)
        lap[pl.ds(start, ROWS), :] = both[:, 0:128]
        for n in range(4):
            packed = both[128 * n : 128 * n + 8, 128:256]
            for i in range(1, 16):
                at = 128 * n + 8 * i
                packed = jnp.where(group == i, both[at : at + 8, 128:256], packed)
            zs[c, pl.ds(8 * n, 8), :] = packed
        for side in range(2):

            @pl.when(has["z", side])
            def _():
                z_copy(side, c, par, 1 - side).start()

    def split(start, new):
        high = new.astype(BF16)
        hl[pl.ds(start, SLAB), 0:128] = high
        hl[pl.ds(start, SLAB), 128:256] = (new - high.astype(F32)).astype(BF16)

    @pl.loop(0, NCH)
    def _(i):
        c = jnp.where(i == 0, flip, jnp.where(i == 1, NCH - 1 - flip, i - 1))

        @pl.loop(0, CHUNK, unroll=4)
        def _(y):
            start = pl.multiple_of(c * ROWS + y * SLAB, SLAB)
            split(start, fld[pl.ds(start + 4 * SLAB, SLAB), :])

        send(c, 0)

    def step(t, carry):
        par = lax.rem(t, 2)
        old, now = (1 - par) * FIELD + 4 * SLAB, par * FIELD + 4 * SLAB

        @pl.when(t < STEPS - 2)
        def _():
            sources(t // 2 + 1, par)

        @pl.loop(0, NCH)
        def _(i):
            c = jnp.where(i == 0, flip, jnp.where(i == 1, NCH - 1 - flip, i - 1))
            first = pl.multiple_of(c * ROWS, ROWS)
            for side in range(2):

                @pl.when(has["y", side] & (c == (0 if side == 0 else NCH - 1)))
                def _():
                    y_wait(side, par)

                @pl.when(has["x", side])
                def _():
                    x_copy(side, c, par, side).wait_recv()
                    rows = pl.ds(pl.multiple_of(c * CHUNK * 4, 64), CHUNK * 4)
                    hb[pl.ds(first + 7 * side, CHUNK * 4, stride=8), :] = xh[par, side, rows, :]

                @pl.when(has["z", side])
                def _():
                    z_copy(side, c, par, side).wait_recv()

            settle(c)

            @pl.loop(0, CHUNK // GROUP)
            def _(y):
                at = pl.multiple_of(y * (GROUP * SLAB), GROUP * SLAB)
                r = pl.multiple_of(first + at, GROUP * SLAB)
                base = pl.multiple_of(now + r, SLAB)
                back = pl.multiple_of(old + r, SLAB)
                mine = pl.ds(pl.multiple_of(y * 8, 8), 8)
                got = jnp.where(lower, zh[par, c, 0, mine, :], zh[par, c, 1, mine, :])
                fresh = []
                for g in range(GROUP):
                    mid = [fld[pl.ds(base + SLAB * g + 8 * j, 8), :] for j in range(4)]
                    edge = [hb[pl.ds(r + SLAB * g + 8 * j, 8), :] for j in range(4)]
                    below = [jnp.where(sub == 0, e, pltpu.roll(v, 1, 0)) for e, v in zip(edge, mid)]
                    above = [jnp.where(sub == 7, e, pltpu.roll(v, 7, 0)) for e, v in zip(edge, mid)]
                    line = below + mid + above
                    tiles = []
                    for j in range(4):
                        spot = SLAB * g + 8 * j
                        total = None
                        for k in range(1, 5):
                            near = (line[4 + j + k] + line[4 + j - k]) + (
                                fld[pl.ds(base + spot + k * SLAB, 8), :]
                                + fld[pl.ds(base + spot - k * SLAB, 8), :]
                            )
                            near = COEF[k] * near
                            total = near if total is None else total + near
                        here = pl.ds(r + spot, 8)
                        turn = (128 - spot) % 128
                        rolled = pltpu.roll(got, turn, 1) if turn else got
                        depth = lap[here, :] + jnp.where(rim, rolled, 0.0)
                        tiles.append(
                            (src[lax.rem(t, 4), here, :] - fld[pl.ds(back + spot, 8), :])
                            + kc[here, :] * mid[j]
                            + hc[here, :] * total
                            + vc[here, :] * depth
                        )
                    fresh.append(jnp.concatenate(tiles, axis=0))
                for g, new in enumerate(fresh):
                    fld[pl.ds(back + SLAB * g, SLAB), :] = new
                    split(pl.multiple_of(r + SLAB * g, SLAB), new)

            @pl.when(t < STEPS - 1)
            def _():
                send(c, 1 - par)

        return carry

    lax.fori_loop(0, STEPS, step, 0)
    for n, mate in mates:
        tell(n, mate, half, gz).wait_send()
    @pl.loop(0, 32, unroll=4)
    def _(y):
        for j in range(4):
            put = pl.ds(j * 32 + y, 8, stride=128)
            take = pl.multiple_of((4 + 32 * half + y) * SLAB + j * 8, 8)
            outp_ref[put, :] = fld[pl.ds(take, 8), :]
            outq_ref[put, :] = fld[pl.ds(take + FIELD, 8), :]


def body(
    pressure, pressure_prev, horiz_coef, vert_coef, traces, recv_cell, recv_owner, trace_counts
):
    coded, peaks = [], []
    for a in (pressure, pressure_prev):
        top = jnp.max(jnp.abs(a), axis=1, keepdims=True)
        top = jnp.where(top > 0.0, top, 1.0)
        coded.append(jnp.round(a * (32767.0 / top)).astype(jnp.int32).astype(jnp.int16))
        peaks.append(top[:, 0])
    coded += [code(horiz_coef), code(vert_coef)]
    coded, peaks = jnp.stack(coded).reshape(4, 1024, 128), jnp.stack(peaks)
    coded, peaks, traces = lax.optimization_barrier((coded, peaks, traces))
    pairs = [(i, i ^ 1) for i in range(lax.axis_size("gy"))]
    other_peak = lax.ppermute(peaks, "gy", pairs)
    other = lax.ppermute(coded, "gy", pairs)

    blocks = [a.reshape(1024, 128) for a in (pressure, pressure_prev, horiz_coef, vert_coef)]

    samples = traces.shape[-1]
    columns, slots = recv_cell.shape[1:]
    per_step = samples // STEPS
    box_table = (
        jnp.arange(samples, dtype=jnp.int32)[:, None] // per_step
        == STEPS - 1 - jnp.arange(STEPS, dtype=jnp.int32)[None, :]
    ).astype(BF16)
    amps = jnp.dot(
        traces.reshape(-1, samples), box_table, preferred_element_type=F32
    ).astype(BF16).reshape(columns, slots, STEPS)
    cell = recv_cell[0]
    x, y, z = cell // 4096, (cell // 128) % 32, cell % 128
    live = jnp.arange(slots, dtype=jnp.int32)[None, :] < trace_counts[0][:, None]
    owner = jnp.where(live, recv_owner[0], -1)
    tags = jnp.stack([y, (x % 4) * 8 + x // 4, z, owner], axis=-1).astype(BF16)
    packed = jnp.concatenate(
        [amps, tags, jnp.zeros((columns, slots, 28), BF16)], axis=-1
    ).reshape(columns, 128)
    routed = lax.all_to_all(packed, ("gx", "gy"), split_axis=0, concat_axis=0, tiled=True)

    vmem = pl.BlockSpec(memory_space=pltpu.VMEM)
    dma = pltpu.SemaphoreType.DMA
    outs = pl.pallas_call(
        kernel,
        out_shape=[jax.ShapeDtypeStruct((1024, 128), F32)] * 2,
        in_specs=[vmem] * 7,
        out_specs=[vmem] * 2,
        scratch_shapes=[
            pltpu.VMEM((2 * FIELD, 128), F32),
            pltpu.VMEM((NY * SLAB, 128), F32),
            pltpu.VMEM((NY * SLAB, 128), F32),
            pltpu.VMEM((NY * SLAB, 128), F32),
            pltpu.VMEM((NY * SLAB, 256), BF16),
            pltpu.VMEM((NY * SLAB, 512), BF16),
            pltpu.VMEM((1024, 128), F32),
            pltpu.VMEM((512, 256), BF16),
            pltpu.VMEM((2, NY * 4, 128), F32),
            pltpu.VMEM((2, 2, NY * 4, 128), F32),
            pltpu.VMEM((NY * SLAB, 128), F32),
            pltpu.VMEM((NCH, 32, 128), F32),
            pltpu.VMEM((2, NCH, 2, 32, 128), F32),
            pltpu.VMEM((4, 1024, 128), F32),
            pltpu.VMEM((2, 4, 64, 128), BF16),
            pltpu.VMEM((256, 256), BF16),
            pltpu.VMEM((NY * SLAB, 128), F32),
            pltpu.VMEM((4, NY * SLAB, 128), F32),
            dma((2,)), dma((2, 2)),
            dma((2, NCH)), dma((2, 2, NCH)),
            dma((2, NCH)), dma((2, 2, NCH)),
            dma((7,)), dma((2, 4)),
        ],
        compiler_params=pltpu.CompilerParams(
            collective_id=0, has_side_effects=True, vmem_limit_bytes=40 * 1024 * 1024
        ),
    )(*blocks, other, other_peak, routed)
    return tuple(o.reshape(32, 32, 128) for o in outs)


def solution(mesh):
    block = P("gx", "gy", "gz")
    placed = (
        block,
        block,
        block,
        block,
        P(("gx", "gy", "gz"), None, None, None),
        P(("gx", "gy", "gz"), None, None),
        P(("gx", "gy", "gz"), None, None),
        P(("gx", "gy", "gz"), None),
    )
    return jax.shard_map(
        body, mesh=mesh, in_specs=placed, out_specs=(block, block), check_vma=False
    )
```

```python
import functools

import jax
import jax.numpy as jnp
from jax import lax
from jax.experimental import pallas as pl
from jax.experimental.pallas import tpu as pltpu
from jax.sharding import PartitionSpec as P

STEPS = 32
MESH = pl.DeviceIdType.MESH
COEF = (-205.0 / 72.0, 8.0 / 5.0, -1.0 / 5.0, 8.0 / 315.0, -1.0 / 560.0)
SCALE = 5040.0
TAPS = (8064.0, -1008.0, 128.0, -9.0)

NY = 64
CHUNK = 16
NCH = NY // CHUNK
ROWS = CHUNK * 32
GROUP = 4
SLAB = 32
FIELD = (NY + 8) * SLAB
F32, BF16 = jnp.float32, jnp.bfloat16


def taps(distance):
    value = jnp.zeros(distance.shape, F32)
    for k in range(1, 5):
        value = jnp.where(distance == k, TAPS[k - 1], value)
    return value


def code(value):
    return jnp.round((value - 0.115) * (32767.0 / 0.075)).astype(jnp.int32).astype(jnp.int16)


def decode(value):
    return value.astype(jnp.int32).astype(F32) * (0.075 / 32767.0) + 0.115


def iota(shape, dim):
    return lax.broadcasted_iota(jnp.int32, shape, dim)


def kernel(
    p_ref, q_ref, h_ref, v_ref, rawcoded, rawpeak, f_ref, outp_ref, outq_ref,
    fld, hc, vc, kc, hl, hot, zhot, wgt, xs, xh, hb, zs, zh, raw, table, band, lap, src,
    ysend, yrecv, xsend, xrecv, zsend, zrecv, tsend, trecv,
):
    gx, gy, gz = lax.axis_index("gx"), lax.axis_index("gy"), lax.axis_index("gz")
    nx, ny, nz = lax.axis_size("gx"), lax.axis_size("gy"), lax.axis_size("gz")
    half = lax.rem(gy, 2)
    partner = gy + 1 - 2 * half
    flip = lax.rem(gy // 2, 2) * (NCH - 1)
    has = {
        ("x", 0): gx > 0, ("x", 1): gx < nx - 1,
        ("y", 0): gy > 1, ("y", 1): gy < ny - 2,
        ("z", 0): gz > 0, ("z", 1): gz < nz - 1,
    }
    peer = {
        ("x", 0): {"gx": gx - 1}, ("x", 1): {"gx": gx + 1},
        ("y", 0): {"gy": gy - 2}, ("y", 1): {"gy": gy + 2},
        ("z", 0): {"gz": gz - 1}, ("z", 1): {"gz": gz + 1},
    }

    def clear(ref, start, count):
        ref[pl.ds(start, count), :] = jnp.zeros((count, 128), F32)

    for par in range(2):
        clear(fld, par * FIELD, 4 * SLAB)
        clear(fld, par * FIELD + (NY + 4) * SLAB, 4 * SLAB)
    zh[...] = jnp.zeros_like(zh)

    mates = [
        (n, {"gy": gy if same else partner, "gz": lax.rem(gz + d, nz)})
        for n, (same, d) in enumerate([(s, d) for s in (True, False) for d in range(nz)][1:])
    ]
    barrier = pltpu.get_barrier_semaphore()
    for _, mate in mates:
        pl.semaphore_signal(barrier, inc=1, device_id=mate, device_id_type=MESH)
    greet = jnp.int32(len(mates))
    for key, ok in has.items():

        @pl.when(ok)
        def _(key=key):
            pl.semaphore_signal(barrier, inc=1, device_id=peer[key], device_id_type=MESH)

        greet = greet + ok.astype(jnp.int32)
    pl.semaphore_wait(barrier, greet)

    def tell(n, mate, col, depth):
        return pltpu.make_async_remote_copy(
            src_ref=f_ref,
            dst_ref=table.at[col, depth],
            send_sem=tsend.at[n],
            recv_sem=trecv.at[col, depth],
            device_id=mate,
            device_id_type=MESH,
        )

    for n, mate in mates:
        tell(n, mate, half, gz).start()
    table[half, gz] = f_ref[...]

    @pl.loop(0, NCH)
    def _(c):
        clear(hb, pl.multiple_of(c * ROWS, ROWS), ROWS)

    depth = lax.rem(iota((256, 128), 0), 128)
    band[:, 0:128] = taps(jnp.abs(depth - iota((256, 128), 1))).astype(BF16)
    m = lax.rem(iota((256, 128), 1), 8)
    band[:, 128:256] = taps(jnp.where(m < 4, 128 + m - depth, depth + 8 - m)).astype(BF16)

    def arrange(refs, first):
        @pl.loop(0, 32, unroll=4)
        def _(y):
            for j in range(4):
                take = pl.ds(j * 32 + y, 8, stride=128)
                put = pl.multiple_of((first + y) * SLAB + j * 8, 8)
                fld[pl.ds(put + 4 * SLAB, 8), :] = refs[0][take, :]
                fld[pl.ds(put + 4 * SLAB + FIELD, 8), :] = refs[1][take, :]
                h, v = refs[2][take, :], refs[3][take, :]
                hc[pl.ds(put, 8), :] = h
                vc[pl.ds(put, 8), :] = v * (1.0 / SCALE)
                kc[pl.ds(put, 8), :] = 2.0 + COEF[0] * (2.0 * h + v)

    arrange((p_ref, q_ref, h_ref, v_ref), 32 * half)
    for n in range(2):
        raw[2 + n] = decode(rawcoded[2 + n])

        @pl.loop(0, 32, unroll=8)
        def _(x):
            rows = pl.ds(pl.multiple_of(x * 32, 32), 32)
            scale = rawpeak[n, pl.ds(x, 1), :] * (1.0 / 32767.0)
            raw[n, rows, :] = rawcoded[n, rows, :].astype(jnp.int32).astype(F32) * scale

    arrange([raw.at[n] for n in range(4)], 32 - 32 * half)

    sub, lane = iota((8, 128), 0), iota((8, 128), 1)
    group = lax.rem((lane + 4) // 8, 16)
    rim = (lane < 4) | (lane >= 124)
    lower = lax.rem(lane, 8) < 4

    def y_copy(side, par):
        src = par * FIELD + (4 if side == 0 else NY) * SLAB
        dst = par * FIELD + (NY + 4 if side == 0 else 0) * SLAB
        return pltpu.make_async_remote_copy(
            src_ref=fld.at[pl.ds(pl.multiple_of(src, 128), 128)],
            dst_ref=fld.at[pl.ds(pl.multiple_of(dst, 128), 128)],
            send_sem=ysend.at[side],
            recv_sem=yrecv.at[1 - side, par],
            device_id=peer["y", side],
            device_id_type=MESH,
        )

    def y_wait(side, par):
        here = pl.ds(pl.multiple_of(par * FIELD + (0 if side == 0 else NY + 4) * SLAB, 128), 128)
        pltpu.make_async_remote_copy(
            src_ref=fld.at[here], dst_ref=fld.at[here], send_sem=ysend.at[side],
            recv_sem=yrecv.at[side, par], device_id=peer["y", side], device_id_type=MESH,
        ).wait_recv()

    def x_copy(side, c, par, there):
        rows = pl.ds(pl.multiple_of(c * CHUNK * 4, 64), CHUNK * 4)
        return pltpu.make_async_remote_copy(
            src_ref=xs.at[side, rows],
            dst_ref=xh.at[par, there, rows],
            send_sem=xsend.at[side, c],
            recv_sem=xrecv.at[there, par, c],
            device_id=peer["x", side],
            device_id_type=MESH,
        )

    def z_copy(side, c, par, there):
        return pltpu.make_async_remote_copy(
            src_ref=zs.at[c],
            dst_ref=zh.at[par, c, there],
            send_sem=zsend.at[side, c],
            recv_sem=zrecv.at[there, par, c],
            device_id=peer["z", side],
            device_id_type=MESH,
        )

    def settle(c):
        for side in range(2):

            @pl.when(has["x", side])
            def _():
                x_copy(side, c, 0, 1 - side).wait_send()

            @pl.when(has["z", side])
            def _():
                z_copy(side, c, 0, 1 - side).wait_send()

            @pl.when(has["y", side] & (c == (0 if side == 0 else NCH - 1)))
            def _():
                y_copy(side, 0).wait_send()

    def send(c, par):
        for side in range(2):

            @pl.when(has["y", side] & (c == (0 if side == 0 else NCH - 1)))
            def _():
                y_copy(side, par).start()

        first = par * FIELD + (4 + c * CHUNK) * SLAB
        rows = pl.ds(pl.multiple_of(c * CHUNK * 4, 64), CHUNK * 4)
        for side in range(2):
            xs[side, rows, :] = fld[pl.ds(first + 7 * side, CHUNK * 4, stride=8), :]

            @pl.when(has["x", side])
            def _():
                x_copy(side, c, par, 1 - side).start()

        start = pl.multiple_of(c * ROWS, ROWS)
        both = jnp.dot(hl[pl.ds(start, ROWS), :], band[...], preferred_element_type=F32)
        lap[pl.ds(start, ROWS), :] = both[:, 0:128]
        for n in range(4):
            packed = both[128 * n : 128 * n + 8, 128:256]
            for i in range(1, 16):
                at = 128 * n + 8 * i
                packed = jnp.where(group == i, both[at : at + 8, 128:256], packed)
            zs[c, pl.ds(8 * n, 8), :] = packed
        for side in range(2):

            @pl.when(has["z", side])
            def _():
                z_copy(side, c, par, 1 - side).start()

    def split(start, new):
        high = new.astype(BF16)
        hl[pl.ds(start, SLAB), 0:128] = high
        hl[pl.ds(start, SLAB), 128:256] = (new - high.astype(F32)).astype(BF16)

    @pl.loop(0, NCH)
    def _(i):
        c = jnp.where(i == 0, flip, jnp.where(i == 1, NCH - 1 - flip, i - 1))

        @pl.loop(0, CHUNK, unroll=4)
        def _(y):
            start = pl.multiple_of(c * ROWS + y * SLAB, SLAB)
            split(start, fld[pl.ds(start + 4 * SLAB, SLAB), :])

        send(c, 0)

    for n, (same, d) in enumerate([(s, d) for s in (True, False) for d in range(nz)][1:]):
        col, depth = half if same else 1 - half, lax.rem(gz + d, nz)
        tell(n, mates[n][1], col, depth).wait_recv()

    for col in range(2):
        packed = table[col].reshape(256, 128)
        for k in range(2):
            pick = iota((8, 128), 1) == 64 * k + 32 + iota((8, 128), 0)
            by_lane = lax.dot_general(
                jnp.where(pick, 1.0, 0.0).astype(BF16), packed,
                (((1,), (1,)), ((), ())), preferred_element_type=F32,
            )
            where = (by_lane[0:1] * 32.0 + by_lane[1:2]).astype(jnp.int32)
            mine = by_lane[3:4].astype(jnp.int32) == gz
            where = jnp.where(mine, where, -1)
            for block in range(4):
                at = iota((256, 256), 0) + block * 256
                hot[pl.ds(col * 1024 + block * 256, 256), pl.ds(k * 256, 256)] = jnp.where(
                    at == where, 1.0, 0.0
                ).astype(BF16)
            spread = jnp.where(iota((128, 128), 0) == 64 * k + 34, 1.0, 0.0).astype(BF16)
            z = jnp.dot(packed, spread, preferred_element_type=F32).astype(jnp.int32)
            zhot[pl.ds(col * 512 + k * 256, 256), :] = jnp.where(
                z == iota((256, 128), 1), 1.0, 0.0
            )

    def sources(u, col):
        for k in range(2):
            when = 64 * k + 2 * u + iota((128, 256), 1) // 128
            spread = jnp.where(iota((128, 256), 0) == when, 1.0, 0.0).astype(BF16)
            amp = jnp.dot(table[col].reshape(256, 128), spread, preferred_element_type=F32)
            at = pl.ds(pl.multiple_of(col * 512 + k * 256, 256), 256)
            wgt[k * 256 : k * 256 + 256, 0:128] = (zhot[at, :] * amp[:, 0:128]).astype(BF16)
            wgt[k * 256 : k * 256 + 256, 128:256] = (zhot[at, :] * amp[:, 128:256]).astype(BF16)
        slot = 2 * lax.rem(u, 2)

        rows = pl.ds(pl.multiple_of(col * 1024, 1024), 1024)
        both = jnp.dot(hot[rows, :], wgt[...], preferred_element_type=F32)
        src[slot, rows, :] = both[:, 0:128]
        src[slot + 1, rows, :] = both[:, 128:256]

    @pl.loop(0, 2)
    def _(col):
        sources(0, col)

    def step(t, carry):
        par = lax.rem(t, 2)
        old, now = (1 - par) * FIELD + 4 * SLAB, par * FIELD + 4 * SLAB

        @pl.when(t < STEPS - 2)
        def _():
            sources(t // 2 + 1, par)

        @pl.loop(0, NCH)
        def _(i):
            c = jnp.where(i == 0, flip, jnp.where(i == 1, NCH - 1 - flip, i - 1))
            first = pl.multiple_of(c * ROWS, ROWS)
            for side in range(2):

                @pl.when(has["y", side] & (c == (0 if side == 0 else NCH - 1)))
                def _():
                    y_wait(side, par)

                @pl.when(has["x", side])
                def _():
                    x_copy(side, c, par, side).wait_recv()
                    rows = pl.ds(pl.multiple_of(c * CHUNK * 4, 64), CHUNK * 4)
                    hb[pl.ds(first + 7 * side, CHUNK * 4, stride=8), :] = xh[par, side, rows, :]

                @pl.when(has["z", side])
                def _():
                    z_copy(side, c, par, side).wait_recv()

            settle(c)

            @pl.loop(0, CHUNK // GROUP)
            def _(y):
                at = pl.multiple_of(y * (GROUP * SLAB), GROUP * SLAB)
                r = pl.multiple_of(first + at, GROUP * SLAB)
                base = pl.multiple_of(now + r, SLAB)
                back = pl.multiple_of(old + r, SLAB)
                mine = pl.ds(pl.multiple_of(y * 8, 8), 8)
                got = jnp.where(lower, zh[par, c, 0, mine, :], zh[par, c, 1, mine, :])
                fresh = []
                for g in range(GROUP):
                    mid = [fld[pl.ds(base + SLAB * g + 8 * j, 8), :] for j in range(4)]
                    edge = [hb[pl.ds(r + SLAB * g + 8 * j, 8), :] for j in range(4)]
                    below = [jnp.where(sub == 0, e, pltpu.roll(v, 1, 0)) for e, v in zip(edge, mid)]
                    above = [jnp.where(sub == 7, e, pltpu.roll(v, 7, 0)) for e, v in zip(edge, mid)]
                    line = below + mid + above
                    tiles = []
                    for j in range(4):
                        spot = SLAB * g + 8 * j
                        total = None
                        for k in range(1, 5):
                            near = (line[4 + j + k] + line[4 + j - k]) + (
                                fld[pl.ds(base + spot + k * SLAB, 8), :]
                                + fld[pl.ds(base + spot - k * SLAB, 8), :]
                            )
                            near = COEF[k] * near
                            total = near if total is None else total + near
                        here = pl.ds(r + spot, 8)
                        turn = (128 - spot) % 128
                        rolled = pltpu.roll(got, turn, 1) if turn else got
                        depth = lap[here, :] + jnp.where(rim, rolled, 0.0)
                        tiles.append(
                            (src[lax.rem(t, 4), here, :] - fld[pl.ds(back + spot, 8), :])
                            + kc[here, :] * mid[j]
                            + hc[here, :] * total
                            + vc[here, :] * depth
                        )
                    fresh.append(jnp.concatenate(tiles, axis=0))
                for g, new in enumerate(fresh):
                    fld[pl.ds(back + SLAB * g, SLAB), :] = new
                    split(pl.multiple_of(r + SLAB * g, SLAB), new)

            @pl.when(t < STEPS - 1)
            def _():
                send(c, 1 - par)

        return carry

    lax.fori_loop(0, STEPS, step, 0)
    for n, mate in mates:
        tell(n, mate, half, gz).wait_send()
    @pl.loop(0, 32, unroll=4)
    def _(y):
        for j in range(4):
            put = pl.ds(j * 32 + y, 8, stride=128)
            take = pl.multiple_of((4 + 32 * half + y) * SLAB + j * 8, 8)
            outp_ref[put, :] = fld[pl.ds(take, 8), :]
            outq_ref[put, :] = fld[pl.ds(take + FIELD, 8), :]


def body(
    pressure, pressure_prev, horiz_coef, vert_coef, traces, recv_cell, recv_owner, trace_counts
):
    coded, peaks = [], []
    for a in (pressure, pressure_prev):
        top = jnp.max(jnp.abs(a), axis=1, keepdims=True)
        top = jnp.where(top > 0.0, top, 1.0)
        coded.append(jnp.round(a * (32767.0 / top)).astype(jnp.int32).astype(jnp.int16))
        peaks.append(top[:, 0])
    coded += [code(horiz_coef), code(vert_coef)]
    coded, peaks = jnp.stack(coded).reshape(4, 1024, 128), jnp.stack(peaks)
    coded, peaks, traces = lax.optimization_barrier((coded, peaks, traces))
    pairs = [(i, i ^ 1) for i in range(lax.axis_size("gy"))]
    other_peak = lax.ppermute(peaks, "gy", pairs)
    other = lax.ppermute(coded, "gy", pairs)

    blocks = [a.reshape(1024, 128) for a in (pressure, pressure_prev, horiz_coef, vert_coef)]

    samples = traces.shape[-1]
    columns, slots = recv_cell.shape[1:]
    per_step = samples // STEPS
    box_table = (
        jnp.arange(samples, dtype=jnp.int32)[:, None] // per_step
        == STEPS - 1 - jnp.arange(STEPS, dtype=jnp.int32)[None, :]
    ).astype(BF16)
    amps = jnp.dot(
        traces.reshape(-1, samples), box_table, preferred_element_type=F32
    ).astype(BF16).reshape(columns, slots, STEPS)
    cell = recv_cell[0]
    x, y, z = cell // 4096, (cell // 128) % 32, cell % 128
    live = jnp.arange(slots, dtype=jnp.int32)[None, :] < trace_counts[0][:, None]
    owner = jnp.where(live, recv_owner[0], -1)
    tags = jnp.stack([y, (x % 4) * 8 + x // 4, z, owner], axis=-1).astype(BF16)
    packed = jnp.concatenate(
        [amps, tags, jnp.zeros((columns, slots, 28), BF16)], axis=-1
    ).reshape(columns, 128)
    routed = lax.all_to_all(packed, ("gx", "gy"), split_axis=0, concat_axis=0, tiled=True)

    vmem = pl.BlockSpec(memory_space=pltpu.VMEM)
    dma = pltpu.SemaphoreType.DMA
    outs = pl.pallas_call(
        kernel,
        out_shape=[jax.ShapeDtypeStruct((1024, 128), F32)] * 2,
        in_specs=[vmem] * 7,
        out_specs=[vmem] * 2,
        scratch_shapes=[
            pltpu.VMEM((2 * FIELD, 128), F32),
            pltpu.VMEM((NY * SLAB, 128), F32),
            pltpu.VMEM((NY * SLAB, 128), F32),
            pltpu.VMEM((NY * SLAB, 128), F32),
            pltpu.VMEM((NY * SLAB, 256), BF16),
            pltpu.VMEM((NY * SLAB, 512), BF16),
            pltpu.VMEM((1024, 128), F32),
            pltpu.VMEM((512, 256), BF16),
            pltpu.VMEM((2, NY * 4, 128), F32),
            pltpu.VMEM((2, 2, NY * 4, 128), F32),
            pltpu.VMEM((NY * SLAB, 128), F32),
            pltpu.VMEM((NCH, 32, 128), F32),
            pltpu.VMEM((2, NCH, 2, 32, 128), F32),
            pltpu.VMEM((4, 1024, 128), F32),
            pltpu.VMEM((2, 4, 64, 128), BF16),
            pltpu.VMEM((256, 256), BF16),
            pltpu.VMEM((NY * SLAB, 128), F32),
            pltpu.VMEM((4, NY * SLAB, 128), F32),
            dma((2,)), dma((2, 2)),
            dma((2, NCH)), dma((2, 2, NCH)),
            dma((2, NCH)), dma((2, 2, NCH)),
            dma((7,)), dma((2, 4)),
        ],
        compiler_params=pltpu.CompilerParams(
            collective_id=0, has_side_effects=True, vmem_limit_bytes=40 * 1024 * 1024
        ),
    )(*blocks, other, other_peak, routed)
    return tuple(o.reshape(32, 32, 128) for o in outs)


def solution(mesh):
    block = P("gx", "gy", "gz")
    placed = (
        block,
        block,
        block,
        block,
        P(("gx", "gy", "gz"), None, None, None),
        P(("gx", "gy", "gz"), None, None),
        P(("gx", "gy", "gz"), None, None),
        P(("gx", "gy", "gz"), None),
    )
    return jax.shard_map(
        body, mesh=mesh, in_specs=placed, out_specs=(block, block), check_vma=False
    )
```
